32 devices in a mesh: tm: 16 (over z, y, core), col: 2 (over x).
Axes of the slice: x: 2, y: 2, z: 4, core: 2. Of those that a mesh axis runs over, the one named last changes fastest.
Arguments:
- design: bfloat16 [2048, 2, 512], P('tm', None, 'col'), may hold values from -512 to 512
- filter_taps: bfloat16 [16, 2, 512], replicated, may hold values from -3 to 3
- segment: int32 [2048], P('tm'), may hold values from 0 to 15, never falling along the last dimension, each value on 1 to 256 neighbouring positions
- valid_flags: int32 [2048], P('tm'), may hold values 0 or 1
- weights: float32 [2, 2048], P(None, 'tm'), may hold values from 0.05 to 20
- block_ids: int32 [2], replicated, may hold values from 0 to 1, each once
Outputs:
- normals: float32 [512, 512], P('tm', 'col')
The draws below stay inside these ranges and needn't reach their ends.
All inputs are finite; a program needn't handle non-finite values. No bound on the sum of `valid_flags` on one device may be relied on, other than what follows from the above.
Results may differ from the reference program's by a relative error of at most 0.0013.
Values may be sent and summed in bfloat16 or wider, within the bound.
No kernel may reach another device: no remote copies, remote signals or barrier semaphores. Data moves between devices by JAX's collectives and lax.ppermute only.
A program may use at most 64 MiB of HBM per device.

```python
import math
import jax
import jax.numpy as jnp
import numpy as np
from jax import lax

CB = 256
TAPS = 512
EP_DEV = 128
EPOCHS = 2048
COLS = 512
SEGS = 16
HB = 4
N_TM = 16
N_COL = 2


def draw_design(key, part):
    key_noise = jax.random.fold_in(key, 11)
    key_pair = jax.random.fold_in(key, 12)
    columns_all = CB * N_COL
    stripe = columns_all // N_TM
    values = jax.random.truncated_normal(key_noise, -6.0, 6.0, (EPOCHS, 2, columns_all), jnp.float32)
    pairing = jax.random.permutation(key_pair, N_TM)
    epoch_block = jnp.arange(EPOCHS) // EP_DEV
    column_block = jnp.arange(columns_all) // stripe
    boosted = pairing[epoch_block][:, None] == column_block[None, :]
    values = values * jnp.where(boosted, 16.0, 1.0)[:, None, :]
    mixed = values + 0.6 * jnp.roll(values, 1, axis=2)
    return mixed.astype(jnp.bfloat16)


def draw_filter_taps(key, part):
    key_base = jax.random.fold_in(key, 21)
    key_scale = jax.random.fold_in(key, 22)
    base = jax.random.truncated_normal(key_base, -6.0, 6.0, (SEGS, 2, TAPS), jnp.float32)
    seg_scale = jnp.exp(jax.random.uniform(key_scale, (SEGS, 2, 1), jnp.float32, math.log(0.5), math.log(2.0)))
    return (base * seg_scale / math.sqrt(TAPS)).astype(jnp.bfloat16)


def plant(entries, key, smallest, largest):
    place = [jax.random.randint(jax.random.fold_in(key, axis), (), 0, length) for axis, length in enumerate(entries.shape)]
    main_axis = entries.shape.index(max(entries.shape))
    neighbour = place[:main_axis] + [(place[main_axis] + 1) % entries.shape[main_axis]] + place[main_axis + 1:]
    return entries.at[tuple(place)].set(smallest).at[tuple(neighbour)].set(largest)


def steps_of(key, shape, cuts, low, top_value):
    gain = 1.0
    for axis_at, shards_of in cuts:
        heights = jax.random.uniform(jax.random.fold_in(jax.random.fold_in(key, 6), axis_at), (shards_of,), jnp.float32, low / len(cuts), top_value / len(cuts))
        gain = gain * jnp.repeat(jnp.exp(heights), shape[axis_at] // shards_of).reshape((-1,) + (1,) * (len(shape) - 1 - axis_at))
    return gain


def length_profile(number_of, total, limit, skew):
    loads = [(1 << 20) // math.isqrt(standing ** skew) + 1 for standing in range(2, number_of + 1)]
    surplus, given = total - limit - (number_of - 1), [1] * (number_of - 1)
    while surplus > 0:
        candidates = [i for i in range(number_of - 1) if given[i] < limit]
        mass, remaining = sum([loads[i] for i in candidates]), surplus
        for i in candidates:
            extra = min(limit - given[i], max(1, remaining * loads[i] // mass), surplus)
            given[i] = given[i] + extra
            surplus = surplus - extra
    return np.array([limit] + given)


def uneven(key, amount, total, limit, lean):
    if amount == 2:
        one = jax.random.randint(key, (), max(1, total - limit), min(limit, total - 1) + 1)
        return jnp.stack([one, total - one])
    lengths = jnp.asarray(length_profile(amount, total, limit, lean), jnp.int32)
    twos = (amount - 1) // 2
    donor, sink = lengths[1:1 + 2 * twos:2], lengths[2:2 + 2 * twos:2]
    slack = jnp.minimum(donor - 1, limit - sink)
    passed = jax.random.randint(jax.random.fold_in(key, 1), (twos,), 0, 1 << 20) % (slack + 1)
    lengths = lengths.at[1:1 + 2 * twos:2].set(donor - passed).at[2:2 + 2 * twos:2].set(sink + passed)
    return lengths[jax.random.permutation(jax.random.fold_in(key, 2), amount)]


def setup_inputs(seed: int = 0) -> dict:
    splits = jax.random.split(jax.random.key(seed), 7)
    return {
        "design": draw_design(jax.random.fold_in(splits[6], 71), 0),
        "filter_taps": draw_filter_taps(jax.random.fold_in(splits[6], 71), 0),
        "segment": jnp.searchsorted(jnp.cumsum(uneven(splits[2], SEGS, EPOCHS, 2 * EP_DEV, 0)), jnp.arange(EPOCHS), side="right").astype(jnp.int32),
        "valid_flags": plant((jax.random.randint(splits[3], (EPOCHS,), 0, 4) < 3).astype(jnp.int32), jax.random.fold_in(splits[3], 1), 0, 1),
        "weights": jnp.clip(jnp.exp(math.log(20.0) - 5.9914645 * jax.random.uniform(splits[4], (2, EPOCHS), jnp.float32) ** steps_of(splits[4], (2, EPOCHS), ((1, 16),), -0.2, 0.2)), 0.05, 20.0),
        "block_ids": jax.random.permutation(splits[5], N_COL).astype(jnp.int32),
    }


def reference(design, filter_taps, segment, valid_flags, weights, block_ids):
    window_rows = (HB + 1) * EP_DEV
    inverse = jnp.argsort(block_ids).astype(jnp.int32)
    padded = jnp.concatenate([jnp.zeros((HB * EP_DEV, 2, COLS), jnp.bfloat16), design], axis=0)
    row_weight = weights * valid_flags.astype(jnp.float32)[None, :]
    out_index = jnp.arange(EP_DEV, dtype=jnp.int32)[:, None]
    in_index = jnp.arange(window_rows, dtype=jnp.int32)[None, :]
    lag_index = HB * EP_DEV + out_index - in_index
    inside = (lag_index >= 0) & (lag_index < TAPS)
    clipped = jnp.clip(lag_index, 0, TAPS - 1).astype(jnp.int32)

    def accumulate(running, block_index):
        first_row = (block_index * EP_DEV).astype(jnp.int32)
        stacked = lax.dynamic_slice_in_dim(padded, first_row, window_rows, 0).astype(jnp.float32)
        segs_here = lax.dynamic_slice_in_dim(segment, first_row, EP_DEV, 0)
        tap_rows = filter_taps[segs_here].astype(jnp.float32)
        gathered = jnp.take_along_axis(tap_rows, jnp.broadcast_to(clipped[:, None, :], (EP_DEV, 2, window_rows)), axis=2)
        toeplitz = jnp.where(inside[:, None, :], gathered, jnp.zeros_like(gathered))
        filtered = jnp.einsum("tks,skc->tkc", toeplitz, stacked, precision=lax.Precision.HIGHEST).astype(jnp.bfloat16)
        ordered = filtered.reshape(EP_DEV, 2, N_COL, CB)[:, :, inverse, :].reshape(EP_DEV, 2, COLS)
        weight_here = lax.dynamic_slice_in_dim(row_weight, first_row, EP_DEV, 1)
        scaled = (ordered.astype(jnp.float32) * weight_here.T[:, :, None]).astype(jnp.bfloat16)
        left = ordered.reshape(2 * EP_DEV, COLS).astype(jnp.float32)
        right = scaled.reshape(2 * EP_DEV, COLS).astype(jnp.float32)
        running = running + jnp.dot(left.T, right, precision=lax.Precision.HIGHEST)
        return running, None

    summed, _ = lax.scan(accumulate, jnp.zeros((COLS, COLS), jnp.float32), jnp.arange(EPOCHS // EP_DEV, dtype=jnp.int32))
    return summed / (2.0 * EPOCHS)
```

```python
import jax
import jax.numpy as jnp
from jax import lax
from jax.sharding import PartitionSpec as P


def body(design, filter_taps, segment, valid_flags, weights, block_ids):
    row_count = design.shape[0]
    block_width = design.shape[2]
    tap_count = filter_taps.shape[2]
    seg_count = filter_taps.shape[0]
    block_count = block_ids.shape[0]
    devices = lax.axis_size("tm")
    columns = lax.axis_size("col")
    halo_depth = (tap_count - 2) // row_count + 1
    odd = lax.axis_index("tm") % 2 == 1
    swap = [(i, i ^ 1) for i in range(devices)]

    blocks = [design] + [None] * halo_depth
    for hop in range(2, halo_depth + 1, 2):
        blocks[hop] = lax.ppermute(design, "tm", [(i, i + hop) for i in range(devices - hop)])
    for hop in range(1, halo_depth + 1, 2):
        after = blocks[hop + 1] if hop + 1 <= halo_depth else blocks[hop - 1]
        blocks[hop] = lax.ppermute(jnp.where(odd, after, blocks[hop - 1]), "tm", swap)

    selector = (segment[:, None] == jnp.arange(seg_count, dtype=jnp.int32)[None, :]).astype(jnp.bfloat16)
    window_rows = (halo_depth + 1) * row_count
    tap_rows = jnp.einsum("ts,skj->ktj", selector, filter_taps, preferred_element_type=jnp.float32).astype(jnp.bfloat16)
    reversed_taps = tap_rows[:, :, ::-1]
    offset = window_rows - row_count - tap_count + 1
    padded = jnp.pad(reversed_taps, ((0, 0), (0, 0), (offset, window_rows + 1 - offset - tap_count)))
    toeplitz = padded.reshape(2, row_count * (window_rows + 1))[:, : row_count * window_rows].reshape(
        2, row_count, window_rows
    )
    filtered = sum(
        jnp.einsum(
            "kts,skc->ktc",
            toeplitz[:, :, (halo_depth - d) * row_count : (halo_depth - d + 1) * row_count],
            blocks[d],
            preferred_element_type=jnp.float32,
        )
        for d in range(halo_depth, -1, -1)
    ).astype(jnp.bfloat16)

    column = lax.axis_index("col")
    held = [filtered]
    for d in range(1, columns):
        held.append(lax.ppermute(filtered, "col", [((c + d) % columns, c) for c in range(columns)]))
    ids = [block_ids[(column + d) % columns] for d in range(columns)]

    def of_parameter(p):
        found = held[0]
        for d in range(1, columns):
            found = jnp.where(ids[d] == p, held[d], found)
        return found

    ordered = jnp.concatenate([of_parameter(p) for p in range(columns)], axis=2)
    row_weight = (weights * valid_flags[None, :].astype(jnp.float32))
    scaled = (of_parameter(column).astype(jnp.float32) * row_weight[:, :, None]).astype(jnp.bfloat16)
    total = jnp.einsum("ktp,ktq->pq", ordered, scaled, preferred_element_type=jnp.float32)
    total = total * (1.0 / (2.0 * row_count * devices))
    parts = total.reshape(devices // 2, 2, -1, block_width)
    even_part, odd_part = parts[:, 0], parts[:, 1]
    mine = jnp.where(odd, odd_part, even_part)
    other = jnp.where(odd, even_part, odd_part)
    mine = mine + lax.ppermute(other, "tm", swap)
    groups = [[2 * c + p for c in range(devices // 2)] for p in range(2)]
    return lax.all_to_all(mine, "tm", 0, 0, axis_index_groups=groups).sum(0)


def solution(mesh):
    return jax.shard_map(
        body,
        mesh=mesh,
        in_specs=(P("tm", None, "col"), P(), P("tm"), P("tm"), P(None, "tm"), P()),
        out_specs=P("tm", "col"),
        check_vma=False,
    )
```

```python
import functools

import jax
import jax.numpy as jnp
from jax import lax
from jax.experimental import pallas as pl
from jax.experimental.pallas import tpu as pltpu
from jax.sharding import PartitionSpec as P

VMEM = pl.BlockSpec(memory_space=pltpu.VMEM)
SMEM = pl.BlockSpec(memory_space=pltpu.SMEM)
FIRST = (((0,), (0,)), ((), ()))
LIMIT = pltpu.CompilerParams(vmem_limit_bytes=24 * 2**20)


def toeplitz_kernel(segment_ref, taps_ref, weights_ref, flags_ref, design_ref, out_ref, row_weight_ref, own_ref):
    own_ref[...] = design_ref[...]
    seg_count = taps_ref.shape[0] // 2
    tap_count = taps_ref.shape[1]
    row_count = segment_ref.shape[1]
    width = out_ref.shape[1]
    halo_rows = width // 2 - row_count
    tile = 128
    tiles = tap_count // tile
    lane = lax.broadcasted_iota(jnp.int32, (tile, 2 * tile), 1)
    row = lax.broadcasted_iota(jnp.int32, (tile, 2 * tile), 0)
    flip = (lane == 2 * (tile - 1 - row)).astype(jnp.float32).astype(jnp.bfloat16)
    seg = lax.broadcasted_iota(jnp.int32, (seg_count, row_count), 0)
    selector = (seg == segment_ref[...]).astype(jnp.float32).astype(jnp.bfloat16)
    column = lax.broadcasted_iota(jnp.int32, (row_count, width), 1)
    first_column = 2 * (halo_rows - lax.axis_index("tm") * row_count)
    row_weight = weights_ref[...] * flags_ref[...].astype(jnp.float32)
    for k in range(2):
        taps = taps_ref[k * seg_count : (k + 1) * seg_count, :]
        pieces = [
            jnp.dot(taps[:, m * tile : (m + 1) * tile], flip, preferred_element_type=jnp.float32)
            for m in range(tiles - 1, -1, -1)
        ]
        pieces.append(jnp.zeros((seg_count, width - 2 * tap_count), jnp.float32))
        spread = pltpu.roll(jnp.concatenate(pieces, axis=1), 2 * (halo_rows - tap_count + 1) + k, 1)
        rows = lax.dot_general(selector, spread.astype(jnp.bfloat16), FIRST, preferred_element_type=jnp.float32)
        rows = pltpu.roll(rows, 0, 1, stride=2, stride_axis=0)
        rows = jnp.where(column >= first_column, rows, 0.0)
        out_ref[k * row_count : (k + 1) * row_count, :] = rows.astype(jnp.bfloat16)
        row_weight_ref[k * row_count : (k + 1) * row_count, :] = jnp.broadcast_to(
            row_weight[k : k + 1, :], (tile, row_count)
        ).T


def filter_kernel(toeplitz_ref, *refs):
    *block_refs, out_ref = refs
    row_count, _, width = block_refs[0].shape
    step = 2 * row_count
    total = None
    for j, block_ref in enumerate(block_refs):
        product = jnp.dot(
            toeplitz_ref[:, j * step : (j + 1) * step],
            block_ref[...].reshape(step, width),
            preferred_element_type=jnp.float32,
        )
        total = product if total is None else total + product
    out_ref[...] = total.astype(jnp.bfloat16)


def gram_kernel(ids_ref, row_weight_ref, *refs):
    *held_refs, mine_ref, other_ref, scaled_ref = refs
    columns = len(held_refs)
    width = held_refs[0].shape[1]
    rows_out = mine_ref.shape[1]
    pairs = width // rows_out // 2
    parity = lax.rem(lax.axis_index("tm"), 2)
    column = lax.axis_index("col")
    ids = [ids_ref[lax.rem(column + d, columns)] for d in range(columns)]
    for d in range(columns):

        @pl.when(ids[d] == column)
        def _(d=d):
            weight = jnp.concatenate([row_weight_ref[...]] * (width // row_weight_ref.shape[1]), axis=1)
            scaled_ref[...] = (held_refs[d][...].astype(jnp.float32) * weight).astype(jnp.bfloat16)

    for d in range(columns):
        product = lax.dot_general(
            held_refs[d][...], scaled_ref[...], FIRST, preferred_element_type=jnp.float32
        ).reshape(pairs, 2, rows_out, width)
        for own in range(2):

            @pl.when(parity == own)
            def _(d=d, own=own, product=product):
                place = pl.ds(ids[d] * pairs, pairs)
                mine_ref[place] = product[:, own]
                other_ref[place] = product[:, 1 - own]


def body(design, filter_taps, segment, valid_flags, weights, block_ids):
    row_count = design.shape[0]
    block_width = design.shape[2]
    tap_count = filter_taps.shape[2]
    seg_count = filter_taps.shape[0]
    devices = lax.axis_size("tm")
    columns = lax.axis_size("col")
    chips = devices // 2
    rows_out = columns * block_width // devices
    halo_depth = (tap_count - 2) // row_count + 1
    index = lax.axis_index("tm")
    odd = index % 2 == 1
    swap = [(i, i ^ 1) for i in range(devices)]

    blocks = [design] + [None] * halo_depth
    for hop in range(2, halo_depth + 1, 2):
        blocks[hop] = lax.ppermute(design, "tm", [(i, (i + hop) % devices) for i in range(devices)])
    toeplitz, row_weight, blocks[0] = pl.pallas_call(
        toeplitz_kernel,
        out_shape=[
            jax.ShapeDtypeStruct((2 * row_count, 2 * (halo_depth + 1) * row_count), jnp.bfloat16),
            jax.ShapeDtypeStruct((2 * row_count, 128), jnp.float32),
            jax.ShapeDtypeStruct(design.shape, design.dtype),
        ],
        in_specs=[VMEM] * 5,
        out_specs=[VMEM] * 3,
        compiler_params=LIMIT,
        name="toeplitz",
    )(
        segment.reshape(1, row_count),
        filter_taps.transpose(1, 0, 2).reshape(2 * seg_count, tap_count),
        weights,
        valid_flags.reshape(1, row_count),
        design,
    )
    for hop in range(1, halo_depth + 1, 2):
        blocks[hop] = lax.ppermute(jnp.where(odd, blocks[hop + 1], blocks[hop - 1]), "tm", swap)
    filtered = pl.pallas_call(
        filter_kernel,
        out_shape=jax.ShapeDtypeStruct((2 * row_count, block_width), jnp.bfloat16),
        in_specs=[VMEM] * (halo_depth + 2),
        out_specs=VMEM,
        compiler_params=LIMIT,
        name="filter",
    )(toeplitz, *blocks[::-1])

    held = [filtered]
    for d in range(1, columns):
        held.append(lax.ppermute(filtered, "col", [((c + d) % columns, c) for c in range(columns)]))
    half = jax.ShapeDtypeStruct((chips, rows_out, block_width), jnp.float32)
    mine, other = pl.pallas_call(
        gram_kernel,
        out_shape=[half, half],
        in_specs=[SMEM] + [VMEM] * (1 + columns),
        out_specs=[VMEM] * 2,
        scratch_shapes=[pltpu.VMEM((2 * row_count, block_width), jnp.bfloat16)],
        compiler_params=LIMIT,
        name="gram",
    )(block_ids, row_weight, *held)

    total = mine + lax.ppermute(other, "tm", swap)
    stride, left = 2, chips
    while left > 1:
        group = 4 if left % 4 == 0 else 2
        shares = total.reshape(left // group, group, rows_out, block_width)
        place = index // stride % group

        def share(j):
            return lax.dynamic_index_in_dim(shares, j, 1, keepdims=False)

        total = share(place)
        for d in (3, 1, 2)[-(group - 1) :] if group == 4 else (1,):
            total = total + lax.ppermute(share(place ^ d), "tm", [(i, i ^ (d * stride)) for i in range(devices)])
        stride, left = stride * group, left // group
    return total[0] * (1.0 / (2.0 * row_count * devices))


def solution(mesh):
    return jax.shard_map(
        body,
        mesh=mesh,
        in_specs=(P("tm", None, "col"), P(), P("tm"), P("tm"), P(None, "tm"), P()),
        out_specs=P("tm", "col"),
        check_vma=False,
    )
```

```python
import functools

import jax
import jax.numpy as jnp
from jax import lax
from jax.experimental import pallas as pl
from jax.experimental.pallas import tpu as pltpu
from jax.sharding import PartitionSpec as P

VMEM = pl.BlockSpec(memory_space=pltpu.VMEM)
SMEM = pl.BlockSpec(memory_space=pltpu.SMEM)
FIRST = (((0,), (0,)), ((), ()))
LIMIT = pltpu.CompilerParams(vmem_limit_bytes=24 * 2**20)


def rows_kernel(weights_ref, flags_ref, segment_ref, rows_ref):
    rows_ref[0:2, :] = weights_ref[...] * flags_ref[...].astype(jnp.float32)
    rows_ref[2:3, :] = segment_ref[...].astype(jnp.float32)
    rows_ref[3:, :] = jnp.zeros_like(rows_ref[3:, :])


def prepare_kernel(taps_ref, design_ref, spread_ref, own_ref):
    own_ref[...] = design_ref[...]
    seg_count, _, tap_count = taps_ref.shape
    width = spread_ref.shape[1]
    row_count = design_ref.shape[0]
    tile = 128
    lane = lax.broadcasted_iota(jnp.int32, (tile, 2 * tile), 1)
    row = lax.broadcasted_iota(jnp.int32, (tile, 2 * tile), 0)
    taps = taps_ref[...].reshape(2 * seg_count, tap_count)
    component = lax.rem(lax.broadcasted_iota(jnp.int32, (2 * seg_count, 2 * tile), 0), 2)
    flips = [(lane == 2 * (tile - 1 - row) + k).astype(jnp.float32).astype(jnp.bfloat16) for k in range(2)]
    pieces = []
    for place in range(tap_count - tile, -1, -tile):
        part = taps[:, place : place + tile]
        first, second = (jnp.dot(part, flip, preferred_element_type=jnp.float32) for flip in flips)
        pieces.append(jnp.where(component == 0, first, second))
    pieces.append(jnp.zeros((2 * seg_count, width - 2 * tap_count), jnp.float32))
    spread = pltpu.roll(jnp.concatenate(pieces, axis=1), width - 2 * row_count - 2 * (tap_count - 1), 1)
    spread_ref[...] = spread.astype(jnp.bfloat16)


def choose_kernel(rows_across_ref, across_ref, own_ref, beside_ref, out_ref):
    out_ref[1] = beside_ref[...]
    index = lax.axis_index("tm")
    both = jnp.bitwise_and(jnp.bitwise_xor(index, lax.div(index, 2)), 1)

    @pl.when(both == 0)
    def _():
        out_ref[0] = across_ref[...]

    @pl.when(both == 1)
    def _():
        out_ref[0] = own_ref[...]


def toeplitz_kernel(rows_ref, rows_across_ref, spread_ref, out_ref, rows_here_ref):
    sources, width = spread_ref.shape
    depth, _, step = out_ref.shape
    row_count = step // 2
    later, epoch_block = epoch_block_here()
    rows = jnp.where(later, rows_across_ref[...], rows_ref[...])
    rows_here_ref[...] = rows
    segment = 2 * rows[2:3, :].astype(jnp.int32)
    source = lax.broadcasted_iota(jnp.int32, (sources, row_count), 0)
    column = lax.broadcasted_iota(jnp.int32, (row_count, width), 1)
    first_column = 2 * ((depth - 1) - epoch_block) * row_count
    for k in range(2):
        selector = (source == segment + k).astype(jnp.float32).astype(jnp.bfloat16)
        shifted = lax.dot_general(selector, spread_ref[...], FIRST, preferred_element_type=jnp.float32)
        shifted = pltpu.roll(shifted, 0, 1, stride=2, stride_axis=0)
        shifted = jnp.where(column >= first_column, shifted, 0.0).astype(jnp.bfloat16)
        for d in range(depth):
            place = (depth - 1 - d) * step
            out_ref[d, k * row_count : (k + 1) * row_count, :] = shifted[:, place : place + step]


def epoch_block_here():
    index, devices = lax.axis_index("tm"), lax.axis_size("tm")
    later = lax.rem(lax.div(index, 2), 2) == 0
    return later, jnp.where(later, lax.rem(index + 4, devices), index)


def filtered_block(toeplitz_ref, beside_ref, own_ref, across_ref, swapped_ref):
    row_count, _, width = own_ref.shape
    step = 2 * row_count
    later, _ = epoch_block_here()
    odd = lax.rem(lax.axis_index("tm"), 2)
    back = jnp.where(later, 4, 0)
    total = None
    for d, block_ref in (
        (2, beside_ref),
        (1 + 2 * odd, swapped_ref.at[1]),
        (back, own_ref),
        (4 - back, across_ref),
        (3 - 2 * odd, swapped_ref.at[0]),
    ):
        product = jnp.dot(
            toeplitz_ref[d], block_ref[...].reshape(step, width), preferred_element_type=jnp.float32
        )
        total = product if total is None else total + product
    return total.T.astype(jnp.bfloat16)


def filter_kernel(toeplitz_ref, beside_ref, own_ref, across_ref, swapped_ref, out_ref):
    block = filtered_block(toeplitz_ref, beside_ref, own_ref, across_ref, swapped_ref)
    out_ref[...] = block.reshape(out_ref.shape)


def filter_split_kernel(
    toeplitz_ref, beside_ref, own_ref, across_ref, swapped_ref, rows_ref, all_ref, here_ref, there_ref
):
    block = filtered_block(toeplitz_ref, beside_ref, own_ref, across_ref, swapped_ref)
    width, length = block.shape
    all_ref[0:width, :] = block
    weight = jnp.concatenate([rows_ref[0:1], rows_ref[1:2]], axis=1)
    high = weight.astype(jnp.bfloat16).astype(jnp.float32)
    middle = (weight - high).astype(jnp.bfloat16).astype(jnp.float32)
    low = weight - high - middle
    line = lax.broadcasted_iota(jnp.int32, (all_ref.shape[0] - width, length), 0)
    spread = jnp.where(line == 0, high, jnp.where(line == 1, middle, jnp.where(line == 2, low, 0.0)))
    all_ref[width:, :] = spread.astype(jnp.bfloat16)
    groups, _, rows_out, _ = here_ref.shape
    block = block.reshape(groups, 2, 2, rows_out, length)
    place = lax.rem(lax.div(lax.axis_index("tm"), 2), 2)
    for side in range(2):

        @pl.when(place == side)
        def _(side=side):
            here_ref[...] = block[:, side]
            there_ref[...] = block[:, 1 - side]


def split_scale_kernel(*refs):
    *held_refs, other_ref, scaled_ref = refs
    width = scaled_ref.shape[1]
    for unit, ref in enumerate(held_refs[:2]):
        lines = ref[width:, :].astype(jnp.float32)
        weight = lines[0:1] + lines[1:2] + lines[2:3]
        scaled_ref[unit] = (ref[0:width, :].astype(jnp.float32) * weight).astype(jnp.bfloat16)
    split_gram(held_refs, scaled_ref, other_ref, 1)


def split_gram_kernel(scaled_ref, *refs):
    *held_refs, mine_ref = refs
    split_gram(held_refs, scaled_ref, mine_ref, 0)


def split_gram(held_refs, scaled_ref, out_ref, flip):
    index, column = lax.axis_index("tm"), lax.axis_index("col")
    place = lax.rem(lax.div(index, 2), 2)
    parity = jnp.bitwise_xor(lax.rem(index, 2), flip)
    all_refs, half_refs = held_refs[:2], held_refs[2:]
    groups, _, rows_out, length = half_refs[0].shape
    first = place * 2 * rows_out + parity * rows_out
    for block in range(2):
        total = None
        for unit in range(2):
            if block == 0:
                pieces = [
                    all_refs[unit][pl.ds(pl.multiple_of(g * 4 * rows_out + first, rows_out), rows_out), :]
                    for g in range(groups)
                ]
                rows = jnp.concatenate(pieces, axis=0)
            else:
                rows = half_refs[unit][:, parity].reshape(groups * rows_out, length)
            product = lax.dot_general(
                rows, scaled_ref[unit], (((1,), (1,)), ((), ())), preferred_element_type=jnp.float32
            )
            total = product if total is None else total + product
        at = jnp.bitwise_xor(column, block) * groups
        out_ref[pl.ds(at, groups)] = total.reshape(groups, rows_out, total.shape[1])


def scale_kernel(ids_ref, rows_ref, rows_beside_ref, *refs):
    *held_refs, other_ref, scaled_ref = refs
    columns = len(held_refs) // 2
    width, length = scaled_ref.shape[1:]
    column = lax.axis_index("col")
    for unit, ref in enumerate((rows_ref, rows_beside_ref)):
        weight = jnp.concatenate([ref[0:1], ref[1:2]], axis=1)
        for d in range(columns):

            @pl.when(ids_ref[lax.rem(column + d, columns)] == column)
            def _(d=d, unit=unit, weight=weight):
                values = held_refs[2 * d + unit][...].reshape(width, length).astype(jnp.float32)
                scaled_ref[unit] = (values * weight).astype(jnp.bfloat16)

    gram(ids_ref, held_refs, scaled_ref, other_ref, 1)


def gram_kernel(ids_ref, scaled_ref, *refs):
    *held_refs, mine_ref = refs
    gram(ids_ref, held_refs, scaled_ref, mine_ref, 0)


def gram(ids_ref, held_refs, scaled_ref, out_ref, flip):
    columns = len(held_refs) // 2
    index, column = lax.axis_index("tm"), lax.axis_index("col")
    beside = lax.rem(lax.div(index, 2), 2)
    parity = jnp.bitwise_xor(lax.rem(index, 2), flip)
    length = scaled_ref.shape[2]
    groups, _, _, rows_out, _ = held_refs[0].shape
    for d in range(columns):
        total = None
        for unit in range(2):
            rows = held_refs[2 * d + unit][:, beside, parity].reshape(groups * rows_out, length)
            product = lax.dot_general(
                rows, scaled_ref[unit], (((1,), (1,)), ((), ())), preferred_element_type=jnp.float32
            )
            total = product if total is None else total + product
        place = pl.ds(ids_ref[lax.rem(column + d, columns)] * groups, groups)
        out_ref[place] = total.reshape(groups, rows_out, total.shape[1])


def body(design, filter_taps, segment, valid_flags, weights, block_ids):
    row_count = design.shape[0]
    block_width = design.shape[2]
    tap_count = filter_taps.shape[2]
    seg_count = filter_taps.shape[0]
    devices = lax.axis_size("tm")
    columns = lax.axis_size("col")
    rows_out = columns * block_width // devices
    halo_depth = (tap_count - 2) // row_count + 1
    if halo_depth != 4 or devices % 4:
        raise ValueError("halo depth")
    index = lax.axis_index("tm")
    swap = [(i, i ^ 1) for i in range(devices)]
    beside_pairs = [(i, i ^ 2) for i in range(devices)]
    across_pairs = [(i, (i + (4 if i & 2 else -4)) % devices) for i in range(devices)]

    across = lax.ppermute(design, "tm", across_pairs)
    rows = pl.pallas_call(
        rows_kernel,
        out_shape=jax.ShapeDtypeStruct((8, row_count), jnp.float32),
        in_specs=[VMEM] * 3,
        out_specs=VMEM,
        compiler_params=LIMIT,
        name="rows",
    )(weights, valid_flags.reshape(1, row_count), segment.reshape(1, row_count))
    rows_pairs = [(i, i ^ 4 if i & 2 else (i - 4) % devices) for i in range(devices)]
    rows_across = lax.ppermute(rows, "tm", rows_pairs)
    beside = lax.ppermute(design, "tm", beside_pairs)
    spread, own = pl.pallas_call(
        prepare_kernel,
        out_shape=[
            jax.ShapeDtypeStruct((2 * seg_count, 2 * (halo_depth + 1) * row_count), jnp.bfloat16),
            jax.ShapeDtypeStruct(design.shape, design.dtype),
        ],
        in_specs=[VMEM] * 2,
        out_specs=[VMEM] * 2,
        compiler_params=LIMIT,
        name="prepare",
    )(filter_taps, design)
    toeplitz, rows_here = pl.pallas_call(
        toeplitz_kernel,
        out_shape=[
            jax.ShapeDtypeStruct((halo_depth + 1, 2 * row_count, 2 * row_count), jnp.bfloat16),
            jax.ShapeDtypeStruct(rows.shape, rows.dtype),
        ],
        in_specs=[VMEM] * 3,
        out_specs=[VMEM] * 2,
        compiler_params=LIMIT,
        name="toeplitz",
    )(rows, rows_across, spread)
    chosen = pl.pallas_call(
        choose_kernel,
        out_shape=jax.ShapeDtypeStruct((2, *design.shape), design.dtype),
        in_specs=[VMEM] * 4,
        out_specs=VMEM,
        compiler_params=LIMIT,
        name="choose",
    )(rows_across, across, own, beside)
    swapped = lax.ppermute(chosen, "tm", swap)
    split = columns == 2 and rows_out % 16 == 0 and block_width % (4 * rows_out) == 0
    finish = finish_two if split else finish_any
    total = finish(toeplitz, rows_here, (beside, own, across, swapped), block_ids, rows_out, swap, beside_pairs)
    return total * (1.0 / (2.0 * row_count * devices))


def core_sum(mine, other, swap):
    return mine + lax.ppermute(other, "tm", swap)


def sum_over_groups(total, stride):
    devices = lax.axis_size("tm")
    index = lax.axis_index("tm")
    left = total.shape[0]
    while left > 1:
        group = 4 if left % 4 == 0 else 2
        shares = total.reshape(left // group, group, *total.shape[1:])
        place = index // stride % group

        def share(j):
            return lax.dynamic_index_in_dim(shares, j, 1, keepdims=False)

        total = share(place)
        for d in (3, 2, 1)[-(group - 1) :]:
            total = total + lax.ppermute(share(place ^ d), "tm", [(i, i ^ (d * stride)) for i in range(devices)])
        stride, left = stride * group, left // group
    return total[0]


def finish_two(toeplitz, rows_here, blocks, block_ids, rows_out, swap, beside_pairs):
    devices = lax.axis_size("tm")
    length, width = toeplitz.shape[1], blocks[0].shape[2]
    groups = width // rows_out // 4
    half = jax.ShapeDtypeStruct((groups, 2, rows_out, length), jnp.bfloat16)
    every, here, there = pl.pallas_call(
        filter_split_kernel,
        out_shape=[jax.ShapeDtypeStruct((width + 16, length), jnp.bfloat16), half, half],
        in_specs=[VMEM] * 6,
        out_specs=[VMEM] * 3,
        compiler_params=LIMIT,
        name="filter",
    )(toeplitz, *blocks, rows_here)

    def sums(own_block):
        def run(every, here, there):
            across_column = [(0, 1), (1, 0)]
            both = [(i * 2 + c, (i ^ 2) * 2 + 1 - c) for i in range(devices) for c in range(2)]
            if own_block:
                held = (
                    every,
                    lax.ppermute(every, "tm", beside_pairs),
                    lax.ppermute(here, "col", across_column),
                    lax.ppermute(there, ("tm", "col"), both),
                )
            else:
                held = (
                    lax.ppermute(every, "col", across_column),
                    lax.ppermute(every, ("tm", "col"), both),
                    here,
                    lax.ppermute(there, "tm", beside_pairs),
                )
            share = jax.ShapeDtypeStruct((2 * groups, rows_out, width), jnp.float32)
            other, scaled = pl.pallas_call(
                split_scale_kernel,
                out_shape=[share, jax.ShapeDtypeStruct((2, width, length), jnp.bfloat16)],
                in_specs=[VMEM] * 4,
                out_specs=[VMEM] * 2,
                compiler_params=LIMIT,
                name="scale",
            )(*held)
            mine = pl.pallas_call(
                split_gram_kernel,
                out_shape=share,
                in_specs=[VMEM] * 5,
                out_specs=VMEM,
                compiler_params=LIMIT,
                name="gram",
            )(scaled, *held)
            return sum_over_groups(core_sum(mine, other, swap), 4)

        return run

    return lax.cond(block_ids[0] == 0, sums(True), sums(False), every, here, there)


def finish_any(toeplitz, rows_here, blocks, block_ids, rows_out, swap, beside_pairs):
    devices, columns = lax.axis_size("tm"), lax.axis_size("col")
    length, width = toeplitz.shape[1], blocks[0].shape[2]
    filtered = pl.pallas_call(
        filter_kernel,
        out_shape=jax.ShapeDtypeStruct((width // rows_out // 4, 2, 2, rows_out, length), jnp.bfloat16),
        in_specs=[VMEM] * 5,
        out_specs=VMEM,
        compiler_params=LIMIT,
        name="filter",
    )(toeplitz, *blocks)
    held = []
    for d in range(columns):
        for e in range(2):
            pairs = [
                (i * columns + (c + d) % columns, (i ^ 2 * e) * columns + c)
                for i in range(devices)
                for c in range(columns)
            ]
            held.append(lax.ppermute(filtered, ("tm", "col"), pairs) if d or e else filtered)
    rows_beside = lax.ppermute(rows_here, "tm", beside_pairs)
    share = jax.ShapeDtypeStruct((devices // 4, rows_out, width), jnp.float32)
    other, scaled = pl.pallas_call(
        scale_kernel,
        out_shape=[share, jax.ShapeDtypeStruct((2, width, length), jnp.bfloat16)],
        in_specs=[SMEM] + [VMEM] * (2 + 2 * columns),
        out_specs=[VMEM] * 2,
        compiler_params=LIMIT,
        name="scale",
    )(block_ids, rows_here, rows_beside, *held)
    mine = pl.pallas_call(
        gram_kernel,
        out_shape=share,
        in_specs=[SMEM] + [VMEM] * (1 + 2 * columns),
        out_specs=VMEM,
        compiler_params=LIMIT,
        name="gram",
    )(block_ids, scaled, *held)
    return sum_over_groups(core_sum(mine, other, swap), 4)


def solution(mesh):
    return jax.shard_map(
        body,
        mesh=mesh,
        in_specs=(P("tm", None, "col"), P(), P("tm"), P("tm"), P(None, "tm"), P()),
        out_specs=P("tm", "col"),
        check_vma=False,
    )
```

```python
import functools

import jax
import jax.numpy as jnp
from jax import lax
from jax.experimental import pallas as pl
from jax.experimental.pallas import tpu as pltpu
from jax.sharding import PartitionSpec as P

VMEM = pl.BlockSpec(memory_space=pltpu.VMEM)
SMEM = pl.BlockSpec(memory_space=pltpu.SMEM)
FIRST = (((0,), (0,)), ((), ()))
LIMIT = pltpu.CompilerParams(vmem_limit_bytes=24 * 2**20)


def rows_kernel(weights_ref, flags_ref, segment_ref, rows_ref):
    rows_ref[0:2, :] = weights_ref[...] * flags_ref[...].astype(jnp.float32)
    rows_ref[2:3, :] = segment_ref[...].astype(jnp.float32)
    rows_ref[3:, :] = jnp.zeros_like(rows_ref[3:, :])


def prepare_kernel(taps_ref, design_ref, spread_ref, own_ref):
    own_ref[...] = design_ref[...]
    seg_count, _, tap_count = taps_ref.shape
    width = spread_ref.shape[1]
    row_count = design_ref.shape[0]
    tile = 128
    lane = lax.broadcasted_iota(jnp.int32, (tile, 2 * tile), 1)
    row = lax.broadcasted_iota(jnp.int32, (tile, 2 * tile), 0)
    taps = taps_ref[...].reshape(2 * seg_count, tap_count)
    component = lax.rem(lax.broadcasted_iota(jnp.int32, (2 * seg_count, 2 * tile), 0), 2)
    flips = [(lane == 2 * (tile - 1 - row) + k).astype(jnp.float32).astype(jnp.bfloat16) for k in range(2)]
    pieces = []
    for place in range(tap_count - tile, -1, -tile):
        part = taps[:, place : place + tile]
        first, second = (jnp.dot(part, flip, preferred_element_type=jnp.float32) for flip in flips)
        pieces.append(jnp.where(component == 0, first, second))
    pieces.append(jnp.zeros((2 * seg_count, width - 2 * tap_count), jnp.float32))
    spread = pltpu.roll(jnp.concatenate(pieces, axis=1), width - 2 * row_count - 2 * (tap_count - 1), 1)
    spread_ref[...] = spread.astype(jnp.bfloat16)


def choose_kernel(rows_across_ref, across_ref, own_ref, beside_ref, out_ref):
    out_ref[1] = beside_ref[...]
    index = lax.axis_index("tm")
    both = jnp.bitwise_and(jnp.bitwise_xor(index, lax.div(index, 2)), 1)

    @pl.when(both == 0)
    def _():
        out_ref[0] = across_ref[...]

    @pl.when(both == 1)
    def _():
        out_ref[0] = own_ref[...]


def toeplitz_kernel(rows_ref, rows_across_ref, spread_ref, out_ref, rows_here_ref):
    sources, width = spread_ref.shape
    depth, _, step = out_ref.shape
    row_count = step // 2
    later, epoch_block = epoch_block_here()
    rows = jnp.where(later, rows_across_ref[...], rows_ref[...])
    rows_here_ref[...] = rows
    segment = 2 * rows[2:3, :].astype(jnp.int32)
    source = lax.broadcasted_iota(jnp.int32, (sources, row_count), 0)
    column = lax.broadcasted_iota(jnp.int32, (row_count, width), 1)
    first_column = 2 * ((depth - 1) - epoch_block) * row_count
    for k in range(2):
        selector = (source == segment + k).astype(jnp.float32).astype(jnp.bfloat16)
        shifted = lax.dot_general(selector, spread_ref[...], FIRST, preferred_element_type=jnp.float32)
        shifted = pltpu.roll(shifted, 0, 1, stride=2, stride_axis=0)
        shifted = jnp.where(column >= first_column, shifted, 0.0).astype(jnp.bfloat16)
        for d in range(depth):
            place = (depth - 1 - d) * step
            out_ref[d, k * row_count : (k + 1) * row_count, :] = shifted[:, place : place + step]


def epoch_block_here():
    index, devices = lax.axis_index("tm"), lax.axis_size("tm")
    later = lax.rem(lax.div(index, 2), 2) == 0
    return later, jnp.where(later, lax.rem(index + 4, devices), index)


def filtered_block(toeplitz_ref, across_ref, own_ref, beside_ref, swapped_ref):
    row_count, _, width = own_ref.shape
    step = 2 * row_count
    later, _ = epoch_block_here()
    odd = lax.rem(lax.axis_index("tm"), 2)
    back = jnp.where(later, 4, 0)
    total = None
    for d, block_ref in (
        (2, beside_ref),
        (1 + 2 * odd, swapped_ref.at[1]),
        (back, own_ref),
        (4 - back, across_ref),
        (3 - 2 * odd, swapped_ref.at[0]),
    ):
        product = jnp.dot(
            toeplitz_ref[d], block_ref[...].reshape(step, width), preferred_element_type=jnp.float32
        )
        total = product if total is None else total + product
    return total.T.astype(jnp.bfloat16)


def filter_kernel(toeplitz_ref, across_ref, own_ref, beside_ref, swapped_ref, out_ref):
    block = filtered_block(toeplitz_ref, across_ref, own_ref, beside_ref, swapped_ref)
    out_ref[...] = block.reshape(out_ref.shape)


def filter_split_kernel(
    toeplitz_ref, across_ref, own_ref, beside_ref, swapped_ref, rows_ref, all_ref, here_ref, there_ref
):
    block = filtered_block(toeplitz_ref, across_ref, own_ref, beside_ref, swapped_ref)
    width, length = block.shape
    all_ref[0:width, :] = block
    weight = jnp.concatenate([rows_ref[0:1], rows_ref[1:2]], axis=1)
    high = weight.astype(jnp.bfloat16).astype(jnp.float32)
    middle = (weight - high).astype(jnp.bfloat16).astype(jnp.float32)
    low = weight - high - middle
    line = lax.broadcasted_iota(jnp.int32, (all_ref.shape[0] - width, length), 0)
    spread = jnp.where(line == 0, high, jnp.where(line == 1, middle, jnp.where(line == 2, low, 0.0)))
    all_ref[width:, :] = spread.astype(jnp.bfloat16)
    groups, _, rows_out, _ = here_ref.shape
    block = block.reshape(groups, 2, 2, rows_out, length)
    place = lax.rem(lax.div(lax.axis_index("tm"), 2), 2)
    for side in range(2):

        @pl.when(place == side)
        def _(side=side):
            here_ref[...] = block[:, side]
            there_ref[...] = block[:, 1 - side]


def split_scale_kernel(*refs):
    *held_refs, other_ref, scaled_ref = refs
    held_refs = [held_refs[i] for i in (3, 2, 1, 0)]
    width = scaled_ref.shape[1]
    for unit, ref in enumerate(held_refs[:2]):
        lines = ref[width:, :].astype(jnp.float32)
        weight = lines[0:1] + lines[1:2] + lines[2:3]
        scaled_ref[unit] = (ref[0:width, :].astype(jnp.float32) * weight).astype(jnp.bfloat16)
    split_gram(held_refs, scaled_ref, other_ref, 1)


def split_gram_kernel(scaled_ref, *refs):
    *held_refs, mine_ref = refs
    held_refs = [held_refs[i] for i in (3, 2, 1, 0)]
    split_gram(held_refs, scaled_ref, mine_ref, 0)


def split_gram(held_refs, scaled_ref, out_ref, flip):
    index, column = lax.axis_index("tm"), lax.axis_index("col")
    place = lax.rem(lax.div(index, 2), 2)
    parity = jnp.bitwise_xor(lax.rem(index, 2), flip)
    all_refs, half_refs = held_refs[:2], held_refs[2:]
    groups, _, rows_out, length = half_refs[0].shape
    first = place * 2 * rows_out + parity * rows_out
    for block in range(2):
        total = None
        for unit in range(2):
            if block == 0:
                pieces = [
                    all_refs[unit][pl.ds(pl.multiple_of(g * 4 * rows_out + first, rows_out), rows_out), :]
                    for g in range(groups)
                ]
                rows = jnp.concatenate(pieces, axis=0)
            else:
                rows = half_refs[unit][:, parity].reshape(groups * rows_out, length)
            product = lax.dot_general(
                rows, scaled_ref[unit], (((1,), (1,)), ((), ())), preferred_element_type=jnp.float32
            )
            total = product if total is None else total + product
        at = jnp.bitwise_xor(column, block) * groups
        out_ref[pl.ds(at, groups)] = total.reshape(groups, rows_out, total.shape[1])


def scale_kernel(ids_ref, rows_ref, rows_beside_ref, *refs):
    *held_refs, other_ref, scaled_ref = refs
    columns = len(held_refs) // 2
    width, length = scaled_ref.shape[1:]
    column = lax.axis_index("col")
    for unit, ref in enumerate((rows_ref, rows_beside_ref)):
        weight = jnp.concatenate([ref[0:1], ref[1:2]], axis=1)
        for d in range(columns):

            @pl.when(ids_ref[lax.rem(column + d, columns)] == column)
            def _(d=d, unit=unit, weight=weight):
                values = held_refs[2 * d + unit][...].reshape(width, length).astype(jnp.float32)
                scaled_ref[unit] = (values * weight).astype(jnp.bfloat16)

    gram(ids_ref, held_refs, scaled_ref, other_ref, 1)


def gram_kernel(ids_ref, scaled_ref, *refs):
    *held_refs, mine_ref = refs
    gram(ids_ref, held_refs, scaled_ref, mine_ref, 0)


def gram(ids_ref, held_refs, scaled_ref, out_ref, flip):
    columns = len(held_refs) // 2
    index, column = lax.axis_index("tm"), lax.axis_index("col")
    beside = lax.rem(lax.div(index, 2), 2)
    parity = jnp.bitwise_xor(lax.rem(index, 2), flip)
    length = scaled_ref.shape[2]
    groups, _, _, rows_out, _ = held_refs[0].shape
    for d in range(columns):
        total = None
        for unit in range(2):
            rows = held_refs[2 * d + unit][:, beside, parity].reshape(groups * rows_out, length)
            product = lax.dot_general(
                rows, scaled_ref[unit], (((1,), (1,)), ((), ())), preferred_element_type=jnp.float32
            )
            total = product if total is None else total + product
        place = pl.ds(ids_ref[lax.rem(column + d, columns)] * groups, groups)
        out_ref[place] = total.reshape(groups, rows_out, total.shape[1])


def body(design, filter_taps, segment, valid_flags, weights, block_ids):
    row_count = design.shape[0]
    block_width = design.shape[2]
    tap_count = filter_taps.shape[2]
    seg_count = filter_taps.shape[0]
    devices = lax.axis_size("tm")
    columns = lax.axis_size("col")
    rows_out = columns * block_width // devices
    halo_depth = (tap_count - 2) // row_count + 1
    if halo_depth != 4 or devices % 4:
        raise ValueError("halo depth")
    index = lax.axis_index("tm")
    swap = [(i, i ^ 1) for i in range(devices)]
    beside_pairs = [(i, i ^ 2) for i in range(devices)]
    across_pairs = [(i, (i + (4 if i & 2 else -4)) % devices) for i in range(devices)]

    across = lax.ppermute(design, "tm", across_pairs)
    rows = pl.pallas_call(
        rows_kernel,
        out_shape=jax.ShapeDtypeStruct((8, row_count), jnp.float32),
        in_specs=[VMEM] * 3,
        out_specs=VMEM,
        compiler_params=LIMIT,
        name="rows",
    )(weights, valid_flags.reshape(1, row_count), segment.reshape(1, row_count))
    rows_pairs = [(i, i ^ 4 if i & 2 else (i - 4) % devices) for i in range(devices)]
    rows_across = lax.ppermute(rows, "tm", rows_pairs)
    beside = lax.ppermute(design, "tm", beside_pairs)
    spread, own = pl.pallas_call(
        prepare_kernel,
        out_shape=[
            jax.ShapeDtypeStruct((2 * seg_count, 2 * (halo_depth + 1) * row_count), jnp.bfloat16),
            jax.ShapeDtypeStruct(design.shape, design.dtype),
        ],
        in_specs=[VMEM] * 2,
        out_specs=[VMEM] * 2,
        compiler_params=LIMIT,
        name="prepare",
    )(filter_taps, design)
    toeplitz, rows_here = pl.pallas_call(
        toeplitz_kernel,
        out_shape=[
            jax.ShapeDtypeStruct((halo_depth + 1, 2 * row_count, 2 * row_count), jnp.bfloat16),
            jax.ShapeDtypeStruct(rows.shape, rows.dtype),
        ],
        in_specs=[VMEM] * 3,
        out_specs=[VMEM] * 2,
        compiler_params=LIMIT,
        name="toeplitz",
    )(rows, rows_across, spread)
    chosen = pl.pallas_call(
        choose_kernel,
        out_shape=jax.ShapeDtypeStruct((2, *design.shape), design.dtype),
        in_specs=[VMEM] * 4,
        out_specs=VMEM,
        compiler_params=LIMIT,
        name="choose",
    )(rows_across, across, own, beside)
    swapped = lax.ppermute(chosen, "tm", swap)
    split = columns == 2 and rows_out % 16 == 0 and block_width % (4 * rows_out) == 0
    finish = finish_two if split else finish_any
    total = finish(toeplitz, rows_here, (across, own, beside, swapped), block_ids, rows_out, swap, beside_pairs)
    return total * (1.0 / (2.0 * row_count * devices))


def core_sum(mine, other, swap):
    return mine + lax.ppermute(other, "tm", swap)


def sum_over_groups(total, stride):
    devices = lax.axis_size("tm")
    index = lax.axis_index("tm")
    left = total.shape[0]
    while left > 1:
        group = 4 if left % 4 == 0 else 2
        shares = total.reshape(left // group, group, *total.shape[1:])
        place = index // stride % group

        def share(j):
            return lax.dynamic_index_in_dim(shares, j, 1, keepdims=False)

        total = share(place)
        for d in (2, 3, 1)[-(group - 1) :]:
            total = total + lax.ppermute(share(place ^ d), "tm", [(i, i ^ (d * stride)) for i in range(devices)])
        stride, left = stride * group, left // group
    return total[0]


def finish_two(toeplitz, rows_here, blocks, block_ids, rows_out, swap, beside_pairs):
    devices = lax.axis_size("tm")
    length, width = toeplitz.shape[1], blocks[0].shape[2]
    groups = width // rows_out // 4
    half = jax.ShapeDtypeStruct((groups, 2, rows_out, length), jnp.bfloat16)
    every, here, there = pl.pallas_call(
        filter_split_kernel,
        out_shape=[jax.ShapeDtypeStruct((width + 16, length), jnp.bfloat16), half, half],
        in_specs=[VMEM] * 6,
        out_specs=[VMEM] * 3,
        compiler_params=LIMIT,
        name="filter",
    )(toeplitz, *blocks, rows_here)

    def sums(own_block):
        def run(every, here, there):
            across_column = [(0, 1), (1, 0)]
            both = [(i * 2 + c, (i ^ 2) * 2 + 1 - c) for i in range(devices) for c in range(2)]
            if own_block:
                held = (
                    every,
                    lax.ppermute(every, "tm", beside_pairs),
                    lax.ppermute(here, "col", across_column),
                    lax.ppermute(there, ("tm", "col"), both),
                )
            else:
                held = (
                    lax.ppermute(every, "col", across_column),
                    lax.ppermute(every, ("tm", "col"), both),
                    here,
                    lax.ppermute(there, "tm", beside_pairs),
                )
            share = jax.ShapeDtypeStruct((2 * groups, rows_out, width), jnp.float32)
            other, scaled = pl.pallas_call(
                split_scale_kernel,
                out_shape=[share, jax.ShapeDtypeStruct((2, width, length), jnp.bfloat16)],
                in_specs=[VMEM] * 4,
                out_specs=[VMEM] * 2,
                compiler_params=LIMIT,
                name="scale",
            )(*(held[i] for i in (3, 2, 1, 0)))
            mine = pl.pallas_call(
                split_gram_kernel,
                out_shape=share,
                in_specs=[VMEM] * 5,
                out_specs=VMEM,
                compiler_params=LIMIT,
                name="gram",
            )(scaled, *(held[i] for i in (3, 2, 1, 0)))
            return sum_over_groups(core_sum(mine, other, swap), 4)

        return run

    return lax.cond(block_ids[0] == 0, sums(True), sums(False), every, here, there)


def finish_any(toeplitz, rows_here, blocks, block_ids, rows_out, swap, beside_pairs):
    devices, columns = lax.axis_size("tm"), lax.axis_size("col")
    length, width = toeplitz.shape[1], blocks[0].shape[2]
    filtered = pl.pallas_call(
        filter_kernel,
        out_shape=jax.ShapeDtypeStruct((width // rows_out // 4, 2, 2, rows_out, length), jnp.bfloat16),
        in_specs=[VMEM] * 5,
        out_specs=VMEM,
        compiler_params=LIMIT,
        name="filter",
    )(toeplitz, *blocks)
    held = []
    for d in range(columns):
        for e in range(2):
            pairs = [
                (i * columns + (c + d) % columns, (i ^ 2 * e) * columns + c)
                for i in range(devices)
                for c in range(columns)
            ]
            held.append(lax.ppermute(filtered, ("tm", "col"), pairs) if d or e else filtered)
    rows_beside = lax.ppermute(rows_here, "tm", beside_pairs)
    share = jax.ShapeDtypeStruct((devices // 4, rows_out, width), jnp.float32)
    other, scaled = pl.pallas_call(
        scale_kernel,
        out_shape=[share, jax.ShapeDtypeStruct((2, width, length), jnp.bfloat16)],
        in_specs=[SMEM] + [VMEM] * (2 + 2 * columns),
        out_specs=[VMEM] * 2,
        compiler_params=LIMIT,
        name="scale",
    )(block_ids, rows_here, rows_beside, *held)
    mine = pl.pallas_call(
        gram_kernel,
        out_shape=share,
        in_specs=[SMEM] + [VMEM] * (1 + 2 * columns),
        out_specs=VMEM,
        compiler_params=LIMIT,
        name="gram",
    )(block_ids, scaled, *held)
    return sum_over_groups(core_sum(mine, other, swap), 4)


def solution(mesh):
    return jax.shard_map(
        body,
        mesh=mesh,
        in_specs=(P("tm", None, "col"), P(), P("tm"), P("tm"), P(None, "tm"), P()),
        out_specs=P("tm", "col"),
        check_vma=False,
    )
```

```python
import functools

import jax
import jax.numpy as jnp
from jax import lax
from jax.experimental import pallas as pl
from jax.experimental.pallas import tpu as pltpu
from jax.sharding import PartitionSpec as P

VMEM = pl.BlockSpec(memory_space=pltpu.VMEM)
SMEM = pl.BlockSpec(memory_space=pltpu.SMEM)
FIRST = (((0,), (0,)), ((), ()))
LIMIT = pltpu.CompilerParams(vmem_limit_bytes=24 * 2**20)
LONG = pl.CostEstimate(flops=2 * 10**10, bytes_accessed=2**20, transcendentals=0)


def rows_kernel(weights_ref, flags_ref, segment_ref, ids_ref, rows_ref, ids_out_ref):
    ids_out_ref[...] = ids_ref[...]
    rows_ref[0:2, :] = weights_ref[...] * flags_ref[...].astype(jnp.float32)
    rows_ref[2:3, :] = segment_ref[...].astype(jnp.float32)
    rows_ref[3:, :] = jnp.zeros_like(rows_ref[3:, :])


def prepare_kernel(taps_ref, design_ref, spread_ref, own_ref):
    own_ref[...] = design_ref[...]
    seg_count, _, tap_count = taps_ref.shape
    width = spread_ref.shape[1]
    row_count = design_ref.shape[0]
    tile = 128
    lane = lax.broadcasted_iota(jnp.int32, (tile, 2 * tile), 1)
    row = lax.broadcasted_iota(jnp.int32, (tile, 2 * tile), 0)
    taps = taps_ref[...].reshape(2 * seg_count, tap_count)
    component = lax.rem(lax.broadcasted_iota(jnp.int32, (2 * seg_count, 2 * tile), 0), 2)
    flips = [(lane == 2 * (tile - 1 - row) + k).astype(jnp.float32).astype(jnp.bfloat16) for k in range(2)]
    pieces = []
    for place in range(tap_count - tile, -1, -tile):
        part = taps[:, place : place + tile]
        first, second = (jnp.dot(part, flip, preferred_element_type=jnp.float32) for flip in flips)
        pieces.append(jnp.where(component == 0, first, second))
    pieces.append(jnp.zeros((2 * seg_count, width - 2 * tap_count), jnp.float32))
    spread = pltpu.roll(jnp.concatenate(pieces, axis=1), width - 2 * row_count - 2 * (tap_count - 1), 1)
    spread_ref[...] = spread.astype(jnp.bfloat16)


def choose_kernel(across_ref, own_ref, beside_ref, out_ref):
    out_ref[1] = beside_ref[...]
    index = lax.axis_index("tm")
    both = jnp.bitwise_and(jnp.bitwise_xor(index, lax.div(index, 2)), 1)

    @pl.when(both == 0)
    def _():
        out_ref[0] = across_ref[...]

    @pl.when(both == 1)
    def _():
        out_ref[0] = own_ref[...]


def toeplitz_kernel(rows_ref, rows_across_ref, spread_ref, out_ref, rows_here_ref):
    sources, width = spread_ref.shape
    depth, _, step = out_ref.shape
    row_count = step // 2
    later, epoch_block = epoch_block_here()
    rows = jnp.where(later, rows_across_ref[...], rows_ref[...])
    rows_here_ref[...] = rows
    segment = 2 * rows[2:3, :].astype(jnp.int32)
    source = lax.broadcasted_iota(jnp.int32, (sources, row_count), 0)
    column = lax.broadcasted_iota(jnp.int32, (row_count, width), 1)
    first_column = 2 * ((depth - 1) - epoch_block) * row_count
    for k in range(2):
        selector = (source == segment + k).astype(jnp.float32).astype(jnp.bfloat16)
        shifted = lax.dot_general(selector, spread_ref[...], FIRST, preferred_element_type=jnp.float32)
        shifted = pltpu.roll(shifted, 0, 1, stride=2, stride_axis=0)
        shifted = jnp.where(column >= first_column, shifted, 0.0).astype(jnp.bfloat16)
        for d in range(depth):
            place = (depth - 1 - d) * step
            out_ref[d, k * row_count : (k + 1) * row_count, :] = shifted[:, place : place + step]


def epoch_block_here():
    index, devices = lax.axis_index("tm"), lax.axis_size("tm")
    later = lax.rem(lax.div(index, 2), 2) == 0
    return later, jnp.where(later, lax.rem(index + 4, devices), index)


def filtered_block(toeplitz_ref, across_ref, own_ref, beside_ref, swapped_ref):
    row_count, _, width = own_ref.shape
    step = 2 * row_count
    later, _ = epoch_block_here()
    odd = lax.rem(lax.axis_index("tm"), 2)
    back = jnp.where(later, 4, 0)
    total = None
    for d, block_ref in (
        (2, beside_ref),
        (1 + 2 * odd, swapped_ref.at[1]),
        (back, own_ref),
        (4 - back, across_ref),
        (3 - 2 * odd, swapped_ref.at[0]),
    ):
        product = jnp.dot(
            toeplitz_ref[d], block_ref[...].reshape(step, width), preferred_element_type=jnp.float32
        )
        total = product if total is None else total + product
    return total.T.astype(jnp.bfloat16)


def filter_kernel(toeplitz_ref, across_ref, own_ref, beside_ref, swapped_ref, out_ref):
    block = filtered_block(toeplitz_ref, across_ref, own_ref, beside_ref, swapped_ref)
    out_ref[...] = block.reshape(out_ref.shape)


def filter_split_kernel(
    toeplitz_ref, beside_ref, own_ref, across_ref, swapped_ref, rows_ref, all_ref, here_ref, there_ref
):
    block = filtered_block(toeplitz_ref, across_ref, own_ref, beside_ref, swapped_ref)
    width, length = block.shape
    all_ref[0:width, :] = block
    weight = jnp.concatenate([rows_ref[0:1], rows_ref[1:2]], axis=1)
    high = weight.astype(jnp.bfloat16).astype(jnp.float32)
    middle = (weight - high).astype(jnp.bfloat16).astype(jnp.float32)
    low = weight - high - middle
    line = lax.broadcasted_iota(jnp.int32, (all_ref.shape[0] - width, length), 0)
    spread = jnp.where(line == 0, high, jnp.where(line == 1, middle, jnp.where(line == 2, low, 0.0)))
    all_ref[width:, :] = spread.astype(jnp.bfloat16)
    groups, _, rows_out, _ = here_ref.shape
    block = block.reshape(groups, 2, 2, rows_out, length)
    place = lax.rem(lax.div(lax.axis_index("tm"), 2), 2)
    for side in range(2):

        @pl.when(place == side)
        def _(side=side):
            here_ref[...] = block[:, side]
            there_ref[...] = block[:, 1 - side]


def split_scale_kernel(back, *refs):
    *held_refs, other_ref, scaled_ref = refs
    held_refs = [held_refs[i] for i in back]
    width = scaled_ref.shape[1]
    for unit, ref in enumerate(held_refs[:2]):
        lines = ref[width:, :].astype(jnp.float32)
        weight = lines[0:1] + lines[1:2] + lines[2:3]
        scaled_ref[unit] = (ref[0:width, :].astype(jnp.float32) * weight).astype(jnp.bfloat16)
    split_gram(held_refs, scaled_ref, other_ref, 1)


def split_gram_kernel(back, scaled_ref, *refs):
    *held_refs, mine_ref = refs
    held_refs = [held_refs[i] for i in back]
    split_gram(held_refs, scaled_ref, mine_ref, 0)


def split_gram(held_refs, scaled_ref, out_ref, flip):
    index, column = lax.axis_index("tm"), lax.axis_index("col")
    place = lax.rem(lax.div(index, 2), 2)
    parity = jnp.bitwise_xor(lax.rem(index, 2), flip)
    all_refs, half_refs = held_refs[:2], held_refs[2:]
    groups, _, rows_out, length = half_refs[0].shape
    first = place * 2 * rows_out + parity * rows_out
    for block in range(2):
        total = None
        for unit in range(2):
            if block == 0:
                pieces = [
                    all_refs[unit][pl.ds(pl.multiple_of(g * 4 * rows_out + first, rows_out), rows_out), :]
                    for g in range(groups)
                ]
                rows = jnp.concatenate(pieces, axis=0)
            else:
                rows = half_refs[unit][:, parity].reshape(groups * rows_out, length)
            product = lax.dot_general(
                rows, scaled_ref[unit], (((1,), (1,)), ((), ())), preferred_element_type=jnp.float32
            )
            total = product if total is None else total + product
        at = jnp.bitwise_xor(column, block) * groups
        out_ref[pl.ds(at, groups)] = total.reshape(groups, rows_out, total.shape[1])


def scale_kernel(ids_ref, rows_ref, rows_beside_ref, *refs):
    *held_refs, other_ref, scaled_ref = refs
    columns = len(held_refs) // 2
    width, length = scaled_ref.shape[1:]
    column = lax.axis_index("col")
    for unit, ref in enumerate((rows_ref, rows_beside_ref)):
        weight = jnp.concatenate([ref[0:1], ref[1:2]], axis=1)
        for d in range(columns):

            @pl.when(ids_ref[lax.rem(column + d, columns)] == column)
            def _(d=d, unit=unit, weight=weight):
                values = held_refs[2 * d + unit][...].reshape(width, length).astype(jnp.float32)
                scaled_ref[unit] = (values * weight).astype(jnp.bfloat16)

    gram(ids_ref, held_refs, scaled_ref, other_ref, 1)


def gram_kernel(ids_ref, scaled_ref, *refs):
    *held_refs, mine_ref = refs
    gram(ids_ref, held_refs, scaled_ref, mine_ref, 0)


def gram(ids_ref, held_refs, scaled_ref, out_ref, flip):
    columns = len(held_refs) // 2
    index, column = lax.axis_index("tm"), lax.axis_index("col")
    beside = lax.rem(lax.div(index, 2), 2)
    parity = jnp.bitwise_xor(lax.rem(index, 2), flip)
    length = scaled_ref.shape[2]
    groups, _, _, rows_out, _ = held_refs[0].shape
    for d in range(columns):
        total = None
        for unit in range(2):
            rows = held_refs[2 * d + unit][:, beside, parity].reshape(groups * rows_out, length)
            product = lax.dot_general(
                rows, scaled_ref[unit], (((1,), (1,)), ((), ())), preferred_element_type=jnp.float32
            )
            total = product if total is None else total + product
        place = pl.ds(ids_ref[lax.rem(column + d, columns)] * groups, groups)
        out_ref[place] = total.reshape(groups, rows_out, total.shape[1])


def body(design, filter_taps, segment, valid_flags, weights, block_ids):
    row_count = design.shape[0]
    block_width = design.shape[2]
    tap_count = filter_taps.shape[2]
    seg_count = filter_taps.shape[0]
    devices = lax.axis_size("tm")
    columns = lax.axis_size("col")
    rows_out = columns * block_width // devices
    halo_depth = (tap_count - 2) // row_count + 1
    if halo_depth != 4 or devices % 4:
        raise ValueError("halo depth")
    index = lax.axis_index("tm")
    swap = [(i, i ^ 1) for i in range(devices)]
    beside_pairs = [(i, i ^ 2) for i in range(devices)]
    across_pairs = [(i, (i + (4 if i & 2 else -4)) % devices) for i in range(devices)]

    across = lax.ppermute(design, "tm", across_pairs)
    rows, ids = pl.pallas_call(
        rows_kernel,
        out_shape=[
            jax.ShapeDtypeStruct((8, row_count), jnp.float32),
            jax.ShapeDtypeStruct((1, columns), jnp.int32),
        ],
        in_specs=[VMEM] * 4,
        out_specs=[VMEM] * 2,
        compiler_params=LIMIT,
        name="rows",
    )(weights, valid_flags.reshape(1, row_count), segment.reshape(1, row_count), block_ids.reshape(1, columns))
    rows_pairs = [(i, i ^ 4 if i & 2 else (i - 4) % devices) for i in range(devices)]
    rows_across = lax.ppermute(rows, "tm", rows_pairs)
    beside = lax.ppermute(design, "tm", beside_pairs)
    spread, own = pl.pallas_call(
        prepare_kernel,
        out_shape=[
            jax.ShapeDtypeStruct((2 * seg_count, 2 * (halo_depth + 1) * row_count), jnp.bfloat16),
            jax.ShapeDtypeStruct(design.shape, design.dtype),
        ],
        in_specs=[VMEM] * 2,
        out_specs=[VMEM] * 2,
        compiler_params=LIMIT,
        name="prepare",
    )(filter_taps, design)
    toeplitz, rows_here = pl.pallas_call(
        toeplitz_kernel,
        out_shape=[
            jax.ShapeDtypeStruct((halo_depth + 1, 2 * row_count, 2 * row_count), jnp.bfloat16),
            jax.ShapeDtypeStruct(rows.shape, rows.dtype),
        ],
        in_specs=[VMEM] * 3,
        out_specs=[VMEM] * 2,
        compiler_params=LIMIT,
        cost_estimate=LONG,
        name="toeplitz",
    )(rows, rows_across, spread)
    chosen = pl.pallas_call(
        choose_kernel,
        out_shape=jax.ShapeDtypeStruct((2, *design.shape), design.dtype),
        in_specs=[VMEM] * 3,
        out_specs=VMEM,
        compiler_params=LIMIT,
        name="choose",
    )(across, own, beside)
    swapped = lax.ppermute(chosen, "tm", swap)
    split = columns == 2 and rows_out % 16 == 0 and block_width % (4 * rows_out) == 0
    finish = finish_two if split else finish_any
    total = finish(toeplitz, rows_here, (across, own, beside, swapped), ids.reshape(columns), rows_out, swap, beside_pairs)
    return total * (1.0 / (2.0 * row_count * devices))


def core_sum(mine, other, swap):
    return mine + lax.ppermute(other, "tm", swap)


def sum_over_groups(total, stride):
    devices = lax.axis_size("tm")
    index = lax.axis_index("tm")
    left = total.shape[0]
    while left > 1:
        group = 4 if left % 4 == 0 else 2
        shares = total.reshape(left // group, group, *total.shape[1:])
        place = index // stride % group

        def share(j):
            return lax.dynamic_index_in_dim(shares, j, 1, keepdims=False)

        total = share(place)
        for d in ((3, 1, 2) if group == 4 else (1,)):
            total = total + lax.ppermute(share(place ^ d), "tm", [(i, i ^ (d * stride)) for i in range(devices)])
        stride, left = stride * group, left // group
    return total[0]


def finish_two(toeplitz, rows_here, blocks, block_ids, rows_out, swap, beside_pairs):
    devices = lax.axis_size("tm")
    length, width = toeplitz.shape[1], blocks[0].shape[2]
    groups = width // rows_out // 4
    half = jax.ShapeDtypeStruct((groups, 2, rows_out, length), jnp.bfloat16)
    every, here, there = pl.pallas_call(
        filter_split_kernel,
        out_shape=[jax.ShapeDtypeStruct((width + 16, length), jnp.bfloat16), half, half],
        in_specs=[VMEM] * 6,
        out_specs=[VMEM] * 3,
        compiler_params=LIMIT,
        name="filter",
    )(toeplitz, blocks[2], blocks[1], blocks[0], blocks[3], rows_here)

    def sums(own_block):
        def run(every, here, there):
            across_column = [(0, 1), (1, 0)]
            both = [(i * 2 + c, (i ^ 2) * 2 + 1 - c) for i in range(devices) for c in range(2)]
            if own_block:
                held = (
                    every,
                    lax.ppermute(every, "tm", beside_pairs),
                    lax.ppermute(here, "col", across_column),
                    lax.ppermute(there, ("tm", "col"), both),
                )
            else:
                held = (
                    lax.ppermute(every, "col", across_column),
                    lax.ppermute(every, ("tm", "col"), both),
                    here,
                    lax.ppermute(there, "tm", beside_pairs),
                )
            order = (1, 3, 2, 0) if own_block else (3, 0, 1, 2)
            back = tuple(order.index(i) for i in range(4))
            share = jax.ShapeDtypeStruct((2 * groups, rows_out, width), jnp.float32)
            other, scaled = pl.pallas_call(
                functools.partial(split_scale_kernel, back),
                out_shape=[share, jax.ShapeDtypeStruct((2, width, length), jnp.bfloat16)],
                in_specs=[VMEM] * 4,
                out_specs=[VMEM] * 2,
                compiler_params=LIMIT,
                name="scale",
            )(*(held[i] for i in order))
            mine = pl.pallas_call(
                functools.partial(split_gram_kernel, back),
                out_shape=share,
                in_specs=[VMEM] * 5,
                out_specs=VMEM,
                compiler_params=LIMIT,
                name="gram",
            )(scaled, *(held[i] for i in order))
            return sum_over_groups(core_sum(mine, other, swap), 4)

        return run

    return lax.cond(block_ids[0] == 0, sums(True), sums(False), every, here, there)


def finish_any(toeplitz, rows_here, blocks, block_ids, rows_out, swap, beside_pairs):
    devices, columns = lax.axis_size("tm"), lax.axis_size("col")
    length, width = toeplitz.shape[1], blocks[0].shape[2]
    filtered = pl.pallas_call(
        filter_kernel,
        out_shape=jax.ShapeDtypeStruct((width // rows_out // 4, 2, 2, rows_out, length), jnp.bfloat16),
        in_specs=[VMEM] * 5,
        out_specs=VMEM,
        compiler_params=LIMIT,
        name="filter",
    )(toeplitz, *blocks)
    held = []
    for d in range(columns):
        for e in range(2):
            pairs = [
                (i * columns + (c + d) % columns, (i ^ 2 * e) * columns + c)
                for i in range(devices)
                for c in range(columns)
            ]
            held.append(lax.ppermute(filtered, ("tm", "col"), pairs) if d or e else filtered)
    rows_beside = lax.ppermute(rows_here, "tm", beside_pairs)
    share = jax.ShapeDtypeStruct((devices // 4, rows_out, width), jnp.float32)
    other, scaled = pl.pallas_call(
        scale_kernel,
        out_shape=[share, jax.ShapeDtypeStruct((2, width, length), jnp.bfloat16)],
        in_specs=[SMEM] + [VMEM] * (2 + 2 * columns),
        out_specs=[VMEM] * 2,
        compiler_params=LIMIT,
        name="scale",
    )(block_ids, rows_here, rows_beside, *held)
    mine = pl.pallas_call(
        gram_kernel,
        out_shape=share,
        in_specs=[SMEM] + [VMEM] * (1 + 2 * columns),
        out_specs=VMEM,
        compiler_params=LIMIT,
        name="gram",
    )(block_ids, scaled, *held)
    return sum_over_groups(core_sum(mine, other, swap), 4)


def solution(mesh):
    return jax.shard_map(
        body,
        mesh=mesh,
        in_specs=(P("tm", None, "col"), P(), P("tm"), P("tm"), P(None, "tm"), P()),
        out_specs=P("tm", "col"),
        check_vma=False,
    )
```

```python
import functools

import jax
import jax.numpy as jnp
from jax import lax
from jax.experimental import pallas as pl
from jax.experimental.pallas import tpu as pltpu
from jax.sharding import PartitionSpec as P

VMEM = pl.BlockSpec(memory_space=pltpu.VMEM)
SMEM = pl.BlockSpec(memory_space=pltpu.SMEM)
FIRST = (((0,), (0,)), ((), ()))
LIMIT = pltpu.CompilerParams(vmem_limit_bytes=24 * 2**20)
LONG = pl.CostEstimate(flops=2 * 10**10, bytes_accessed=2**20, transcendentals=0)


def rows_kernel(weights_ref, flags_ref, segment_ref, ids_ref, rows_ref, ids_out_ref):
    ids_out_ref[...] = ids_ref[...]
    rows_ref[0:2, :] = weights_ref[...] * flags_ref[...].astype(jnp.float32)
    rows_ref[2:3, :] = segment_ref[...].astype(jnp.float32)
    rows_ref[3:, :] = jnp.zeros_like(rows_ref[3:, :])


def prepare_kernel(taps_ref, design_ref, spread_ref, own_ref):
    own_ref[...] = design_ref[...]
    seg_count, _, tap_count = taps_ref.shape
    width = spread_ref.shape[1]
    row_count = design_ref.shape[0]
    tile = 128
    lane = lax.broadcasted_iota(jnp.int32, (tile, 2 * tile), 1)
    row = lax.broadcasted_iota(jnp.int32, (tile, 2 * tile), 0)
    taps = taps_ref[...].reshape(2 * seg_count, tap_count)
    component = lax.rem(lax.broadcasted_iota(jnp.int32, (2 * seg_count, 2 * tile), 0), 2)
    flips = [(lane == 2 * (tile - 1 - row) + k).astype(jnp.float32).astype(jnp.bfloat16) for k in range(2)]
    pieces = []
    for place in range(tap_count - tile, -1, -tile):
        part = taps[:, place : place + tile]
        first, second = (jnp.dot(part, flip, preferred_element_type=jnp.float32) for flip in flips)
        pieces.append(jnp.where(component == 0, first, second))
    pieces.append(jnp.zeros((2 * seg_count, width - 2 * tap_count), jnp.float32))
    spread = pltpu.roll(jnp.concatenate(pieces, axis=1), width - 2 * row_count - 2 * (tap_count - 1), 1)
    spread_ref[...] = spread.astype(jnp.bfloat16)


def choose_kernel(across_ref, own_ref, beside_ref, out_ref):
    out_ref[1] = beside_ref[...]
    index = lax.axis_index("tm")
    both = jnp.bitwise_and(jnp.bitwise_xor(index, lax.div(index, 2)), 1)

    @pl.when(both == 0)
    def _():
        out_ref[0] = across_ref[...]

    @pl.when(both == 1)
    def _():
        out_ref[0] = own_ref[...]


def toeplitz_kernel(rows_ref, rows_across_ref, spread_ref, out_ref, rows_here_ref):
    sources, width = spread_ref.shape
    depth, _, step = out_ref.shape
    row_count = step // 2
    later, epoch_block = epoch_block_here()
    rows = jnp.where(later, rows_across_ref[...], rows_ref[...])
    rows_here_ref[...] = rows
    segment = 2 * rows[2:3, :].astype(jnp.int32)
    source = lax.broadcasted_iota(jnp.int32, (sources, row_count), 0)
    column = lax.broadcasted_iota(jnp.int32, (row_count, width), 1)
    first_column = 2 * ((depth - 1) - epoch_block) * row_count
    for k in range(2):
        selector = (source == segment + k).astype(jnp.float32).astype(jnp.bfloat16)
        shifted = lax.dot_general(selector, spread_ref[...], FIRST, preferred_element_type=jnp.float32)
        shifted = pltpu.roll(shifted, 0, 1, stride=2, stride_axis=0)
        shifted = jnp.where(column >= first_column, shifted, 0.0).astype(jnp.bfloat16)
        for d in range(depth):
            place = (depth - 1 - d) * step
            out_ref[d, k * row_count : (k + 1) * row_count, :] = shifted[:, place : place + step]


def epoch_block_here():
    index, devices = lax.axis_index("tm"), lax.axis_size("tm")
    later = lax.rem(lax.div(index, 2), 2) == 0
    return later, jnp.where(later, lax.rem(index + 4, devices), index)


def sum_products(toeplitz_ref, pairs, total=None):
    for d, block_ref in pairs:
        row_count, _, width = block_ref.shape
        block = block_ref[...].reshape(2 * row_count, width)
        product = jnp.dot(toeplitz_ref[d], block, preferred_element_type=jnp.float32)
        total = product if total is None else total + product
    return total


def partial_kernel(toeplitz_ref, beside_ref, own_ref, across_ref, out_ref):
    later, _ = epoch_block_here()
    back = jnp.where(later, 4, 0)
    out_ref[...] = sum_products(toeplitz_ref, ((2, beside_ref), (back, own_ref), (4 - back, across_ref)))


def filtered_block(partial_ref, toeplitz_ref, swapped_ref):
    odd = lax.rem(lax.axis_index("tm"), 2)
    pairs = ((1 + 2 * odd, swapped_ref.at[1]), (3 - 2 * odd, swapped_ref.at[0]))
    return sum_products(toeplitz_ref, pairs, partial_ref[...]).astype(jnp.bfloat16).T


def filter_kernel(partial_ref, toeplitz_ref, swapped_ref, out_ref):
    block = filtered_block(partial_ref, toeplitz_ref, swapped_ref)
    out_ref[...] = block.reshape(out_ref.shape)


def filter_split_kernel(partial_ref, toeplitz_ref, swapped_ref, rows_ref, all_ref, here_ref, there_ref):
    block = filtered_block(partial_ref, toeplitz_ref, swapped_ref)
    width, length = block.shape
    all_ref[0:width, :] = block
    weight = jnp.concatenate([rows_ref[0:1], rows_ref[1:2]], axis=1)
    high = weight.astype(jnp.bfloat16).astype(jnp.float32)
    middle = (weight - high).astype(jnp.bfloat16).astype(jnp.float32)
    low = weight - high - middle
    line = lax.broadcasted_iota(jnp.int32, (all_ref.shape[0] - width, length), 0)
    spread = jnp.where(line == 0, high, jnp.where(line == 1, middle, jnp.where(line == 2, low, 0.0)))
    all_ref[width:, :] = spread.astype(jnp.bfloat16)
    groups, _, rows_out, _ = here_ref.shape
    block = block.reshape(groups, 2, 2, rows_out, length)
    place = lax.rem(lax.div(lax.axis_index("tm"), 2), 2)
    for side in range(2):

        @pl.when(place == side)
        def _(side=side):
            here_ref[...] = block[:, side]
            there_ref[...] = block[:, 1 - side]


def split_scale_kernel(back, *refs):
    *held_refs, other_ref, scaled_ref = refs
    held_refs = [held_refs[i] for i in back]
    width = scaled_ref.shape[1]
    for unit, ref in enumerate(held_refs[:2]):
        lines = ref[width:, :].astype(jnp.float32)
        weight = lines[0:1] + lines[1:2] + lines[2:3]
        scaled_ref[unit] = (ref[0:width, :].astype(jnp.float32) * weight).astype(jnp.bfloat16)
    split_gram(held_refs, scaled_ref, other_ref, 1)


def split_gram_kernel(back, scaled_ref, *refs):
    *held_refs, mine_ref = refs
    held_refs = [held_refs[i] for i in back]
    split_gram(held_refs, scaled_ref, mine_ref, 0)


def split_gram(held_refs, scaled_ref, out_ref, flip):
    index, column = lax.axis_index("tm"), lax.axis_index("col")
    place = lax.rem(lax.div(index, 2), 2)
    parity = jnp.bitwise_xor(lax.rem(index, 2), flip)
    all_refs, half_refs = held_refs[:2], held_refs[2:]
    groups, _, rows_out, length = half_refs[0].shape
    first = place * 2 * rows_out + parity * rows_out
    for block in range(2):
        total = None
        for unit in range(2):
            if block == 0:
                pieces = [
                    all_refs[unit][pl.ds(pl.multiple_of(g * 4 * rows_out + first, rows_out), rows_out), :]
                    for g in range(groups)
                ]
                rows = jnp.concatenate(pieces, axis=0)
            else:
                rows = half_refs[unit][:, parity].reshape(groups * rows_out, length)
            product = lax.dot_general(
                rows, scaled_ref[unit], (((1,), (1,)), ((), ())), preferred_element_type=jnp.float32
            )
            total = product if total is None else total + product
        at = jnp.bitwise_xor(column, block) * groups
        out_ref[pl.ds(at, groups)] = total.reshape(groups, rows_out, total.shape[1])


def scale_kernel(ids_ref, rows_ref, rows_beside_ref, *refs):
    *held_refs, other_ref, scaled_ref = refs
    columns = len(held_refs) // 2
    width, length = scaled_ref.shape[1:]
    column = lax.axis_index("col")
    for unit, ref in enumerate((rows_ref, rows_beside_ref)):
        weight = jnp.concatenate([ref[0:1], ref[1:2]], axis=1)
        for d in range(columns):

            @pl.when(ids_ref[lax.rem(column + d, columns)] == column)
            def _(d=d, unit=unit, weight=weight):
                values = held_refs[2 * d + unit][...].reshape(width, length).astype(jnp.float32)
                scaled_ref[unit] = (values * weight).astype(jnp.bfloat16)

    gram(ids_ref, held_refs, scaled_ref, other_ref, 1)


def gram_kernel(ids_ref, scaled_ref, *refs):
    *held_refs, mine_ref = refs
    gram(ids_ref, held_refs, scaled_ref, mine_ref, 0)


def gram(ids_ref, held_refs, scaled_ref, out_ref, flip):
    columns = len(held_refs) // 2
    index, column = lax.axis_index("tm"), lax.axis_index("col")
    beside = lax.rem(lax.div(index, 2), 2)
    parity = jnp.bitwise_xor(lax.rem(index, 2), flip)
    length = scaled_ref.shape[2]
    groups, _, _, rows_out, _ = held_refs[0].shape
    for d in range(columns):
        total = None
        for unit in range(2):
            rows = held_refs[2 * d + unit][:, beside, parity].reshape(groups * rows_out, length)
            product = lax.dot_general(
                rows, scaled_ref[unit], (((1,), (1,)), ((), ())), preferred_element_type=jnp.float32
            )
            total = product if total is None else total + product
        place = pl.ds(ids_ref[lax.rem(column + d, columns)] * groups, groups)
        out_ref[place] = total.reshape(groups, rows_out, total.shape[1])


def body(design, filter_taps, segment, valid_flags, weights, block_ids):
    row_count = design.shape[0]
    block_width = design.shape[2]
    tap_count = filter_taps.shape[2]
    seg_count = filter_taps.shape[0]
    devices = lax.axis_size("tm")
    columns = lax.axis_size("col")
    rows_out = columns * block_width // devices
    halo_depth = (tap_count - 2) // row_count + 1
    if halo_depth != 4 or devices % 4:
        raise ValueError("halo depth")
    index = lax.axis_index("tm")
    swap = [(i, i ^ 1) for i in range(devices)]
    beside_pairs = [(i, i ^ 2) for i in range(devices)]
    across_pairs = [(i, (i + (4 if i & 2 else -4)) % devices) for i in range(devices)]

    across = lax.ppermute(design, "tm", across_pairs)
    rows, ids = pl.pallas_call(
        rows_kernel,
        out_shape=[
            jax.ShapeDtypeStruct((8, row_count), jnp.float32),
            jax.ShapeDtypeStruct((1, columns), jnp.int32),
        ],
        in_specs=[VMEM] * 4,
        out_specs=[VMEM] * 2,
        compiler_params=LIMIT,
        name="rows",
    )(weights, valid_flags.reshape(1, row_count), segment.reshape(1, row_count), block_ids.reshape(1, columns))
    rows_pairs = [(i, i ^ 4 if i & 2 else (i - 4) % devices) for i in range(devices)]
    rows_across = lax.ppermute(rows, "tm", rows_pairs)
    beside = lax.ppermute(design, "tm", beside_pairs)
    spread, own = pl.pallas_call(
        prepare_kernel,
        out_shape=[
            jax.ShapeDtypeStruct((2 * seg_count, 2 * (halo_depth + 1) * row_count), jnp.bfloat16),
            jax.ShapeDtypeStruct(design.shape, design.dtype),
        ],
        in_specs=[VMEM] * 2,
        out_specs=[VMEM] * 2,
        compiler_params=LIMIT,
        name="prepare",
    )(filter_taps, design)
    toeplitz, rows_here = pl.pallas_call(
        toeplitz_kernel,
        out_shape=[
            jax.ShapeDtypeStruct((halo_depth + 1, 2 * row_count, 2 * row_count), jnp.bfloat16),
            jax.ShapeDtypeStruct(rows.shape, rows.dtype),
        ],
        in_specs=[VMEM] * 3,
        out_specs=[VMEM] * 2,
        compiler_params=LIMIT,
        cost_estimate=LONG,
        name="toeplitz",
    )(rows, rows_across, spread)
    chosen = pl.pallas_call(
        choose_kernel,
        out_shape=jax.ShapeDtypeStruct((2, *design.shape), design.dtype),
        in_specs=[VMEM] * 3,
        out_specs=VMEM,
        compiler_params=LIMIT,
        name="choose",
    )(across, own, beside)
    swapped = lax.ppermute(chosen, "tm", swap)
    partial = pl.pallas_call(
        partial_kernel,
        out_shape=jax.ShapeDtypeStruct((2 * row_count, block_width), jnp.float32),
        in_specs=[VMEM] * 4,
        out_specs=VMEM,
        compiler_params=LIMIT,
        name="partial",
    )(toeplitz, beside, own, across)
    split = columns == 2 and rows_out % 16 == 0 and block_width % (4 * rows_out) == 0
    finish = finish_two if split else finish_any
    total = finish(rows_here, (partial, toeplitz, swapped), ids.reshape(columns), rows_out, swap, beside_pairs)
    return total * (1.0 / (2.0 * row_count * devices))


def core_sum(mine, other, swap):
    return mine + lax.ppermute(other, "tm", swap)


def sum_over_groups(total, stride):
    devices = lax.axis_size("tm")
    index = lax.axis_index("tm")
    left = total.shape[0]
    while left > 1:
        group = 4 if left % 4 == 0 else 2
        shares = total.reshape(left // group, group, *total.shape[1:])
        place = index // stride % group

        def share(j):
            return lax.dynamic_index_in_dim(shares, j, 1, keepdims=False)

        total = share(place)
        for d in ((3, 1, 2) if group == 4 else (1,)):
            total = total + lax.ppermute(share(place ^ d), "tm", [(i, i ^ (d * stride)) for i in range(devices)])
        stride, left = stride * group, left // group
    return total[0]


def finish_two(rows_here, blocks, block_ids, rows_out, swap, beside_pairs):
    devices = lax.axis_size("tm")
    length, width = blocks[0].shape
    groups = width // rows_out // 4
    half = jax.ShapeDtypeStruct((groups, 2, rows_out, length), jnp.bfloat16)
    every, here, there = pl.pallas_call(
        filter_split_kernel,
        out_shape=[jax.ShapeDtypeStruct((width + 16, length), jnp.bfloat16), half, half],
        in_specs=[VMEM] * 4,
        out_specs=[VMEM] * 3,
        compiler_params=LIMIT,
        name="filter",
    )(*blocks, rows_here)

    def sums(own_block):
        def run(every, here, there):
            across_column = [(0, 1), (1, 0)]
            both = [(i * 2 + c, (i ^ 2) * 2 + 1 - c) for i in range(devices) for c in range(2)]
            if own_block:
                held = (
                    every,
                    lax.ppermute(every, "tm", beside_pairs),
                    lax.ppermute(here, "col", across_column),
                    lax.ppermute(there, ("tm", "col"), both),
                )
            else:
                held = (
                    lax.ppermute(every, "col", across_column),
                    lax.ppermute(every, ("tm", "col"), both),
                    here,
                    lax.ppermute(there, "tm", beside_pairs),
                )
            order = (1, 3, 2, 0) if own_block else (3, 0, 1, 2)
            back = tuple(order.index(i) for i in range(4))
            share = jax.ShapeDtypeStruct((2 * groups, rows_out, width), jnp.float32)
            other, scaled = pl.pallas_call(
                functools.partial(split_scale_kernel, back),
                out_shape=[share, jax.ShapeDtypeStruct((2, width, length), jnp.bfloat16)],
                in_specs=[VMEM] * 4,
                out_specs=[VMEM] * 2,
                compiler_params=LIMIT,
                name="scale",
            )(*(held[i] for i in order))
            mine = pl.pallas_call(
                functools.partial(split_gram_kernel, back),
                out_shape=share,
                in_specs=[VMEM] * 5,
                out_specs=VMEM,
                compiler_params=LIMIT,
                name="gram",
            )(scaled, *(held[i] for i in order))
            return sum_over_groups(core_sum(mine, other, swap), 4)

        return run

    return lax.cond(block_ids[0] == 0, sums(True), sums(False), every, here, there)


def finish_any(rows_here, blocks, block_ids, rows_out, swap, beside_pairs):
    devices, columns = lax.axis_size("tm"), lax.axis_size("col")
    length, width = blocks[0].shape
    filtered = pl.pallas_call(
        filter_kernel,
        out_shape=jax.ShapeDtypeStruct((width // rows_out // 4, 2, 2, rows_out, length), jnp.bfloat16),
        in_specs=[VMEM] * 3,
        out_specs=VMEM,
        compiler_params=LIMIT,
        name="filter",
    )(*blocks)
    held = []
    for d in range(columns):
        for e in range(2):
            pairs = [
                (i * columns + (c + d) % columns, (i ^ 2 * e) * columns + c)
                for i in range(devices)
                for c in range(columns)
            ]
            held.append(lax.ppermute(filtered, ("tm", "col"), pairs) if d or e else filtered)
    rows_beside = lax.ppermute(rows_here, "tm", beside_pairs)
    share = jax.ShapeDtypeStruct((devices // 4, rows_out, width), jnp.float32)
    other, scaled = pl.pallas_call(
        scale_kernel,
        out_shape=[share, jax.ShapeDtypeStruct((2, width, length), jnp.bfloat16)],
        in_specs=[SMEM] + [VMEM] * (2 + 2 * columns),
        out_specs=[VMEM] * 2,
        compiler_params=LIMIT,
        name="scale",
    )(block_ids, rows_here, rows_beside, *held)
    mine = pl.pallas_call(
        gram_kernel,
        out_shape=share,
        in_specs=[SMEM] + [VMEM] * (1 + 2 * columns),
        out_specs=VMEM,
        compiler_params=LIMIT,
        name="gram",
    )(block_ids, scaled, *held)
    return sum_over_groups(core_sum(mine, other, swap), 4)


def solution(mesh):
    return jax.shard_map(
        body,
        mesh=mesh,
        in_specs=(P("tm", None, "col"), P(), P("tm"), P("tm"), P(None, "tm"), P()),
        out_specs=P("tm", "col"),
        check_vma=False,
    )
```

```python
import functools

import jax
import jax.numpy as jnp
from jax import lax
from jax.experimental import pallas as pl
from jax.experimental.pallas import tpu as pltpu
from jax.sharding import PartitionSpec as P

VMEM = pl.BlockSpec(memory_space=pltpu.VMEM)
SMEM = pl.BlockSpec(memory_space=pltpu.SMEM)
FIRST = (((0,), (0,)), ((), ()))
LIMIT = pltpu.CompilerParams(vmem_limit_bytes=24 * 2**20)
LONG = pl.CostEstimate(flops=2 * 10**10, bytes_accessed=2**20, transcendentals=0)


def rows_kernel(weights_ref, flags_ref, segment_ref, ids_ref, rows_ref, ids_out_ref):
    ids_out_ref[...] = ids_ref[...]
    rows_ref[0:2, :] = weights_ref[...] * flags_ref[...].astype(jnp.float32)
    rows_ref[2:3, :] = segment_ref[...].astype(jnp.float32)
    rows_ref[3:, :] = jnp.zeros_like(rows_ref[3:, :])


def prepare_kernel(taps_ref, design_ref, spread_ref, own_ref):
    own_ref[...] = design_ref[...]
    seg_count, _, tap_count = taps_ref.shape
    width = spread_ref.shape[1]
    row_count = design_ref.shape[0]
    tile = 128
    lane = lax.broadcasted_iota(jnp.int32, (tile, 2 * tile), 1)
    row = lax.broadcasted_iota(jnp.int32, (tile, 2 * tile), 0)
    taps = taps_ref[...].reshape(2 * seg_count, tap_count)
    component = lax.rem(lax.broadcasted_iota(jnp.int32, (2 * seg_count, 2 * tile), 0), 2)
    flips = [(lane == 2 * (tile - 1 - row) + k).astype(jnp.float32).astype(jnp.bfloat16) for k in range(2)]
    pieces = []
    for place in range(tap_count - tile, -1, -tile):
        part = taps[:, place : place + tile]
        first, second = (jnp.dot(part, flip, preferred_element_type=jnp.float32) for flip in flips)
        pieces.append(jnp.where(component == 0, first, second))
    pieces.append(jnp.zeros((2 * seg_count, width - 2 * tap_count), jnp.float32))
    spread = pltpu.roll(jnp.concatenate(pieces, axis=1), width - 2 * row_count - 2 * (tap_count - 1), 1)
    spread_ref[...] = spread.astype(jnp.bfloat16)


def choose_kernel(across_ref, own_ref, beside_ref, out_ref):
    out_ref[1] = beside_ref[...]
    index = lax.axis_index("tm")
    both = jnp.bitwise_and(jnp.bitwise_xor(index, lax.div(index, 2)), 1)

    @pl.when(both == 0)
    def _():
        out_ref[0] = across_ref[...]

    @pl.when(both == 1)
    def _():
        out_ref[0] = own_ref[...]


def toeplitz_kernel(rows_ref, rows_across_ref, spread_ref, out_ref, rows_here_ref):
    sources, width = spread_ref.shape
    depth, _, step = out_ref.shape
    row_count = step // 2
    later, epoch_block = epoch_block_here()
    rows = jnp.where(later, rows_across_ref[...], rows_ref[...])
    rows_here_ref[...] = rows
    segment = 2 * rows[2:3, :].astype(jnp.int32)
    source = lax.broadcasted_iota(jnp.int32, (sources, row_count), 0)
    column = lax.broadcasted_iota(jnp.int32, (row_count, width), 1)
    first_column = 2 * ((depth - 1) - epoch_block) * row_count
    for k in range(2):
        selector = (source == segment + k).astype(jnp.float32).astype(jnp.bfloat16)
        shifted = lax.dot_general(selector, spread_ref[...], FIRST, preferred_element_type=jnp.float32)
        shifted = pltpu.roll(shifted, 0, 1, stride=2, stride_axis=0)
        shifted = jnp.where(column >= first_column, shifted, 0.0).astype(jnp.bfloat16)
        for d in range(depth):
            place = (depth - 1 - d) * step
            out_ref[d, k * row_count : (k + 1) * row_count, :] = shifted[:, place : place + step]


def epoch_block_here():
    index, devices = lax.axis_index("tm"), lax.axis_size("tm")
    later = lax.rem(lax.div(index, 2), 2) == 0
    return later, jnp.where(later, lax.rem(index + 4, devices), index)


def sum_products(toeplitz_ref, pairs, total=None):
    for d, block_ref in pairs:
        row_count, _, width = block_ref.shape
        block = block_ref[...].reshape(2 * row_count, width)
        product = jnp.dot(toeplitz_ref[d], block, preferred_element_type=jnp.float32)
        total = product if total is None else total + product
    return total


def partial_kernel(toeplitz_ref, beside_ref, own_ref, across_ref, out_ref):
    later, _ = epoch_block_here()
    back = jnp.where(later, 4, 0)
    out_ref[...] = sum_products(toeplitz_ref, ((2, beside_ref), (back, own_ref), (4 - back, across_ref)))


def filtered_block(partial_ref, toeplitz_ref, swapped_ref):
    odd = lax.rem(lax.axis_index("tm"), 2)
    pairs = ((1 + 2 * odd, swapped_ref.at[1]), (3 - 2 * odd, swapped_ref.at[0]))
    return sum_products(toeplitz_ref, pairs, partial_ref[...]).astype(jnp.bfloat16).T


def filter_kernel(partial_ref, toeplitz_ref, swapped_ref, out_ref):
    block = filtered_block(partial_ref, toeplitz_ref, swapped_ref)
    out_ref[...] = block.reshape(out_ref.shape)


def filter_split_kernel(partial_ref, toeplitz_ref, swapped_ref, all_ref, here_ref, there_ref):
    block = filtered_block(partial_ref, toeplitz_ref, swapped_ref)
    width, length = block.shape
    all_ref[...] = block
    groups, _, rows_out, _ = here_ref.shape
    block = block.reshape(groups, 2, 2, rows_out, length)
    place = lax.rem(lax.div(lax.axis_index("tm"), 2), 2)
    for side in range(2):

        @pl.when(place == side)
        def _(side=side):
            here_ref[...] = block[:, side]
            there_ref[...] = block[:, 1 - side]


def split_scale_kernel(back, *refs):
    *held_refs, rows_ref, rows_beside_ref, other_ref, scaled_ref = refs
    held_refs = [held_refs[i] for i in back]
    for unit, (ref, lines_ref) in enumerate(zip(held_refs[:2], (rows_ref, rows_beside_ref))):
        weight = jnp.concatenate([lines_ref[0:1], lines_ref[1:2]], axis=1)
        scaled_ref[unit] = (ref[...].astype(jnp.float32) * weight).astype(jnp.bfloat16)
    split_gram(held_refs, scaled_ref, other_ref, 1)


def split_gram_kernel(back, scaled_ref, *refs):
    *held_refs, mine_ref = refs
    held_refs = [held_refs[i] for i in back]
    split_gram(held_refs, scaled_ref, mine_ref, 0)


def split_gram(held_refs, scaled_ref, out_ref, flip):
    index, column = lax.axis_index("tm"), lax.axis_index("col")
    place = lax.rem(lax.div(index, 2), 2)
    parity = jnp.bitwise_xor(lax.rem(index, 2), flip)
    all_refs, half_refs = held_refs[:2], held_refs[2:]
    groups, _, rows_out, length = half_refs[0].shape
    first = place * 2 * rows_out + parity * rows_out
    for block in range(2):
        total = None
        for unit in range(2):
            if block == 0:
                pieces = [
                    all_refs[unit][pl.ds(pl.multiple_of(g * 4 * rows_out + first, rows_out), rows_out), :]
                    for g in range(groups)
                ]
                rows = jnp.concatenate(pieces, axis=0)
            else:
                rows = half_refs[unit][:, parity].reshape(groups * rows_out, length)
            product = lax.dot_general(
                rows, scaled_ref[unit], (((1,), (1,)), ((), ())), preferred_element_type=jnp.float32
            )
            total = product if total is None else total + product
        at = jnp.bitwise_xor(column, block) * groups
        out_ref[pl.ds(at, groups)] = total.reshape(groups, rows_out, total.shape[1])


def scale_kernel(ids_ref, rows_ref, rows_beside_ref, *refs):
    *held_refs, other_ref, scaled_ref = refs
    columns = len(held_refs) // 2
    width, length = scaled_ref.shape[1:]
    column = lax.axis_index("col")
    for unit, ref in enumerate((rows_ref, rows_beside_ref)):
        weight = jnp.concatenate([ref[0:1], ref[1:2]], axis=1)
        for d in range(columns):

            @pl.when(ids_ref[lax.rem(column + d, columns)] == column)
            def _(d=d, unit=unit, weight=weight):
                values = held_refs[2 * d + unit][...].reshape(width, length).astype(jnp.float32)
                scaled_ref[unit] = (values * weight).astype(jnp.bfloat16)

    gram(ids_ref, held_refs, scaled_ref, other_ref, 1)


def gram_kernel(ids_ref, scaled_ref, *refs):
    *held_refs, mine_ref = refs
    gram(ids_ref, held_refs, scaled_ref, mine_ref, 0)


def gram(ids_ref, held_refs, scaled_ref, out_ref, flip):
    columns = len(held_refs) // 2
    index, column = lax.axis_index("tm"), lax.axis_index("col")
    beside = lax.rem(lax.div(index, 2), 2)
    parity = jnp.bitwise_xor(lax.rem(index, 2), flip)
    length = scaled_ref.shape[2]
    groups, _, _, rows_out, _ = held_refs[0].shape
    for d in range(columns):
        total = None
        for unit in range(2):
            rows = held_refs[2 * d + unit][:, beside, parity].reshape(groups * rows_out, length)
            product = lax.dot_general(
                rows, scaled_ref[unit], (((1,), (1,)), ((), ())), preferred_element_type=jnp.float32
            )
            total = product if total is None else total + product
        place = pl.ds(ids_ref[lax.rem(column + d, columns)] * groups, groups)
        out_ref[place] = total.reshape(groups, rows_out, total.shape[1])


def body(design, filter_taps, segment, valid_flags, weights, block_ids):
    row_count = design.shape[0]
    block_width = design.shape[2]
    tap_count = filter_taps.shape[2]
    seg_count = filter_taps.shape[0]
    devices = lax.axis_size("tm")
    columns = lax.axis_size("col")
    rows_out = columns * block_width // devices
    halo_depth = (tap_count - 2) // row_count + 1
    if halo_depth != 4 or devices % 4:
        raise ValueError("halo depth")
    index = lax.axis_index("tm")
    swap = [(i, i ^ 1) for i in range(devices)]
    beside_pairs = [(i, i ^ 2) for i in range(devices)]
    across_pairs = [(i, (i + (4 if i & 2 else -4)) % devices) for i in range(devices)]

    across = lax.ppermute(design, "tm", across_pairs)
    rows, ids = pl.pallas_call(
        rows_kernel,
        out_shape=[
            jax.ShapeDtypeStruct((8, row_count), jnp.float32),
            jax.ShapeDtypeStruct((1, columns), jnp.int32),
        ],
        in_specs=[VMEM] * 4,
        out_specs=[VMEM] * 2,
        compiler_params=LIMIT,
        name="rows",
    )(weights, valid_flags.reshape(1, row_count), segment.reshape(1, row_count), block_ids.reshape(1, columns))
    rows_pairs = [(i, i ^ 4 if i & 2 else (i - 4) % devices) for i in range(devices)]
    rows_across = lax.ppermute(rows, "tm", rows_pairs)
    beside = lax.ppermute(design, "tm", beside_pairs)
    spread, own = pl.pallas_call(
        prepare_kernel,
        out_shape=[
            jax.ShapeDtypeStruct((2 * seg_count, 2 * (halo_depth + 1) * row_count), jnp.bfloat16),
            jax.ShapeDtypeStruct(design.shape, design.dtype),
        ],
        in_specs=[VMEM] * 2,
        out_specs=[VMEM] * 2,
        compiler_params=LIMIT,
        name="prepare",
    )(filter_taps, design)
    toeplitz, rows_here = pl.pallas_call(
        toeplitz_kernel,
        out_shape=[
            jax.ShapeDtypeStruct((halo_depth + 1, 2 * row_count, 2 * row_count), jnp.bfloat16),
            jax.ShapeDtypeStruct(rows.shape, rows.dtype),
        ],
        in_specs=[VMEM] * 3,
        out_specs=[VMEM] * 2,
        compiler_params=LIMIT,
        cost_estimate=LONG,
        name="toeplitz",
    )(rows, rows_across, spread)
    chosen = pl.pallas_call(
        choose_kernel,
        out_shape=jax.ShapeDtypeStruct((2, *design.shape), design.dtype),
        in_specs=[VMEM] * 3,
        out_specs=VMEM,
        compiler_params=LIMIT,
        name="choose",
    )(across, own, beside)
    swapped = lax.ppermute(chosen, "tm", swap)
    partial = pl.pallas_call(
        partial_kernel,
        out_shape=jax.ShapeDtypeStruct((2 * row_count, block_width), jnp.float32),
        in_specs=[VMEM] * 4,
        out_specs=VMEM,
        compiler_params=LIMIT,
        name="partial",
    )(toeplitz, beside, own, across)
    split = columns == 2 and rows_out % 16 == 0 and block_width % (4 * rows_out) == 0
    finish = finish_two if split else finish_any
    total = finish(rows_here, (partial, toeplitz, swapped), ids.reshape(columns), rows_out, swap, beside_pairs)
    return total * (1.0 / (2.0 * row_count * devices))


def core_sum(mine, other, swap):
    return mine + lax.ppermute(other, "tm", swap)


def sum_over_groups(total, stride, turns=(3, 1, 2)):
    devices = lax.axis_size("tm")
    index = lax.axis_index("tm")
    left = total.shape[0]
    while left > 1:
        group = 4 if left % 4 == 0 else 2
        shares = total.reshape(left // group, group, *total.shape[1:])
        place = index // stride % group

        def share(j):
            return lax.dynamic_index_in_dim(shares, j, 1, keepdims=False)

        total = share(place)
        for d in turns if group == 4 else (1,):
            total = total + lax.ppermute(share(place ^ d), "tm", [(i, i ^ (d * stride)) for i in range(devices)])
        stride, left = stride * group, left // group
    return total[0]


def finish_two(rows_here, blocks, block_ids, rows_out, swap, beside_pairs):
    devices = lax.axis_size("tm")
    length, width = blocks[0].shape
    groups = width // rows_out // 4
    half = jax.ShapeDtypeStruct((groups, 2, rows_out, length), jnp.bfloat16)
    every, here, there = pl.pallas_call(
        filter_split_kernel,
        out_shape=[jax.ShapeDtypeStruct((width, length), jnp.bfloat16), half, half],
        in_specs=[VMEM] * 3,
        out_specs=[VMEM] * 3,
        compiler_params=LIMIT,
        name="filter",
    )(*blocks)

    def sums(own_block):
        def run(every, here, there, rows_here):
            across_column = [(0, 1), (1, 0)]
            both = [(i * 2 + c, (i ^ 2) * 2 + 1 - c) for i in range(devices) for c in range(2)]
            if own_block:
                held = (
                    every,
                    lax.ppermute(every, "tm", beside_pairs),
                    lax.ppermute(here, "col", across_column),
                    lax.ppermute(there, ("tm", "col"), both),
                )
            else:
                held = (
                    lax.ppermute(every, "col", across_column),
                    lax.ppermute(every, ("tm", "col"), both),
                    here,
                    lax.ppermute(there, "tm", beside_pairs),
                )
            order = (1, 3, 2, 0) if own_block else (3, 0, 1, 2)
            back = tuple(order.index(i) for i in range(4))
            share = jax.ShapeDtypeStruct((2 * groups, rows_out, width), jnp.float32)
            other, scaled = pl.pallas_call(
                functools.partial(split_scale_kernel, back),
                out_shape=[share, jax.ShapeDtypeStruct((2, width, length), jnp.bfloat16)],
                in_specs=[VMEM] * 6,
                out_specs=[VMEM] * 2,
                compiler_params=LIMIT,
                name="scale",
            )(*(held[i] for i in order), rows_here, lax.ppermute(rows_here, "tm", beside_pairs))
            mine = pl.pallas_call(
                functools.partial(split_gram_kernel, back),
                out_shape=share,
                in_specs=[VMEM] * 5,
                out_specs=VMEM,
                compiler_params=LIMIT,
                name="gram",
            )(scaled, *(held[i] for i in order))
            return sum_over_groups(core_sum(mine, other, swap), 4, (2, 1, 3) if own_block else (3, 1, 2))

        return run

    return lax.cond(block_ids[0] == 0, sums(True), sums(False), every, here, there, rows_here)


def finish_any(rows_here, blocks, block_ids, rows_out, swap, beside_pairs):
    devices, columns = lax.axis_size("tm"), lax.axis_size("col")
    length, width = blocks[0].shape
    filtered = pl.pallas_call(
        filter_kernel,
        out_shape=jax.ShapeDtypeStruct((width // rows_out // 4, 2, 2, rows_out, length), jnp.bfloat16),
        in_specs=[VMEM] * 3,
        out_specs=VMEM,
        compiler_params=LIMIT,
        name="filter",
    )(*blocks)
    held = []
    for d in range(columns):
        for e in range(2):
            pairs = [
                (i * columns + (c + d) % columns, (i ^ 2 * e) * columns + c)
                for i in range(devices)
                for c in range(columns)
            ]
            held.append(lax.ppermute(filtered, ("tm", "col"), pairs) if d or e else filtered)
    rows_beside = lax.ppermute(rows_here, "tm", beside_pairs)
    share = jax.ShapeDtypeStruct((devices // 4, rows_out, width), jnp.float32)
    other, scaled = pl.pallas_call(
        scale_kernel,
        out_shape=[share, jax.ShapeDtypeStruct((2, width, length), jnp.bfloat16)],
        in_specs=[SMEM] + [VMEM] * (2 + 2 * columns),
        out_specs=[VMEM] * 2,
        compiler_params=LIMIT,
        name="scale",
    )(block_ids, rows_here, rows_beside, *held)
    mine = pl.pallas_call(
        gram_kernel,
        out_shape=share,
        in_specs=[SMEM] + [VMEM] * (1 + 2 * columns),
        out_specs=VMEM,
        compiler_params=LIMIT,
        name="gram",
    )(block_ids, scaled, *held)
    return sum_over_groups(core_sum(mine, other, swap), 4)


def solution(mesh):
    return jax.shard_map(
        body,
        mesh=mesh,
        in_specs=(P("tm", None, "col"), P(), P("tm"), P("tm"), P(None, "tm"), P()),
        out_specs=P("tm", "col"),
        check_vma=False,
    )
```

```python
import functools

import jax
import jax.numpy as jnp
from jax import lax
from jax.experimental import pallas as pl
from jax.experimental.pallas import tpu as pltpu
from jax.sharding import PartitionSpec as P

VMEM = pl.BlockSpec(memory_space=pltpu.VMEM)
SMEM = pl.BlockSpec(memory_space=pltpu.SMEM)
FIRST = (((0,), (0,)), ((), ()))
LIMIT = pltpu.CompilerParams(vmem_limit_bytes=24 * 2**20)
LONG = pl.CostEstimate(flops=2 * 10**10, bytes_accessed=2**20, transcendentals=0)


def rows_kernel(weights_ref, flags_ref, segment_ref, ids_ref, rows_ref, ids_out_ref):
    ids_out_ref[...] = ids_ref[...]
    rows_ref[0:2, :] = weights_ref[...] * flags_ref[...].astype(jnp.float32)
    rows_ref[2:3, :] = segment_ref[...].astype(jnp.float32)
    rows_ref[3:, :] = jnp.zeros_like(rows_ref[3:, :])


def prepare_kernel(taps_ref, design_ref, spread_ref, own_ref):
    own_ref[...] = design_ref[...]
    seg_count, _, tap_count = taps_ref.shape
    width = spread_ref.shape[1]
    row_count = design_ref.shape[0]
    tile = 128
    lane = lax.broadcasted_iota(jnp.int32, (tile, 2 * tile), 1)
    row = lax.broadcasted_iota(jnp.int32, (tile, 2 * tile), 0)
    taps = taps_ref[...].reshape(2 * seg_count, tap_count)
    component = lax.rem(lax.broadcasted_iota(jnp.int32, (2 * seg_count, 2 * tile), 0), 2)
    flips = [(lane == 2 * (tile - 1 - row) + k).astype(jnp.float32).astype(jnp.bfloat16) for k in range(2)]
    pieces = []
    for place in range(tap_count - tile, -1, -tile):
        part = taps[:, place : place + tile]
        first, second = (jnp.dot(part, flip, preferred_element_type=jnp.float32) for flip in flips)
        pieces.append(jnp.where(component == 0, first, second))
    pieces.append(jnp.zeros((2 * seg_count, width - 2 * tap_count), jnp.float32))
    spread = pltpu.roll(jnp.concatenate(pieces, axis=1), width - 2 * row_count - 2 * (tap_count - 1), 1)
    spread_ref[...] = spread.astype(jnp.bfloat16)


def choose_kernel(across_ref, own_ref, beside_ref, out_ref):
    out_ref[1] = beside_ref[...]
    index = lax.axis_index("tm")
    both = jnp.bitwise_and(jnp.bitwise_xor(index, lax.div(index, 2)), 1)

    @pl.when(both == 0)
    def _():
        out_ref[0] = across_ref[...]

    @pl.when(both == 1)
    def _():
        out_ref[0] = own_ref[...]


def toeplitz_kernel(rows_ref, rows_across_ref, spread_ref, out_ref, rows_here_ref):
    sources, width = spread_ref.shape
    depth, _, step = out_ref.shape
    row_count = step // 2
    later, epoch_block = epoch_block_here()
    rows = jnp.where(later, rows_across_ref[...], rows_ref[...])
    rows_here_ref[...] = rows
    segment = 2 * rows[2:3, :].astype(jnp.int32)
    source = lax.broadcasted_iota(jnp.int32, (sources, row_count), 0)
    column = lax.broadcasted_iota(jnp.int32, (row_count, width), 1)
    first_column = 2 * ((depth - 1) - epoch_block) * row_count
    for k in range(2):
        selector = (source == segment + k).astype(jnp.float32).astype(jnp.bfloat16)
        shifted = lax.dot_general(selector, spread_ref[...], FIRST, preferred_element_type=jnp.float32)
        shifted = pltpu.roll(shifted, 0, 1, stride=2, stride_axis=0)
        shifted = jnp.where(column >= first_column, shifted, 0.0).astype(jnp.bfloat16)
        for d in range(depth):
            place = (depth - 1 - d) * step
            out_ref[d, k * row_count : (k + 1) * row_count, :] = shifted[:, place : place + step]


def epoch_block_here():
    index, devices = lax.axis_index("tm"), lax.axis_size("tm")
    later = lax.rem(lax.div(index, 2), 2) == 0
    return later, jnp.where(later, lax.rem(index + 4, devices), index)


def sum_products(toeplitz_ref, pairs, total=None):
    for d, block_ref in pairs:
        row_count, _, width = block_ref.shape
        block = block_ref[...].reshape(2 * row_count, width)
        product = jnp.dot(toeplitz_ref[d], block, preferred_element_type=jnp.float32)
        total = product if total is None else total + product
    return total


def partial_kernel(toeplitz_ref, beside_ref, own_ref, across_ref, out_ref):
    later, _ = epoch_block_here()
    back = jnp.where(later, 4, 0)
    out_ref[...] = sum_products(toeplitz_ref, ((2, beside_ref), (back, own_ref), (4 - back, across_ref)))


def filtered_block(partial_ref, toeplitz_ref, swapped_ref):
    odd = lax.rem(lax.axis_index("tm"), 2)
    pairs = ((1 + 2 * odd, swapped_ref.at[1]), (3 - 2 * odd, swapped_ref.at[0]))
    return sum_products(toeplitz_ref, pairs, partial_ref[...]).astype(jnp.bfloat16).T


def filter_kernel(partial_ref, toeplitz_ref, swapped_ref, out_ref):
    block = filtered_block(partial_ref, toeplitz_ref, swapped_ref)
    out_ref[...] = block.reshape(out_ref.shape)


def filter_split_kernel(partial_ref, toeplitz_ref, swapped_ref, all_ref, here_ref, there_ref):
    block = filtered_block(partial_ref, toeplitz_ref, swapped_ref)
    width, length = block.shape
    all_ref[...] = block
    groups, _, rows_out, _ = here_ref.shape
    block = block.reshape(groups, 2, 2, rows_out, length)
    place = lax.rem(lax.div(lax.axis_index("tm"), 2), 2)
    for side in range(2):

        @pl.when(place == side)
        def _(side=side):
            here_ref[...] = block[:, side]
            there_ref[...] = block[:, 1 - side]


def split_scale_kernel(back, *refs):
    *held_refs, rows_ref, rows_beside_ref, other_ref, scaled_ref = refs
    held_refs = [held_refs[i] for i in back]
    for unit, (ref, lines_ref) in enumerate(zip(held_refs[:2], (rows_ref, rows_beside_ref))):
        weight = jnp.concatenate([lines_ref[0:1], lines_ref[1:2]], axis=1)
        scaled_ref[unit] = (ref[...].astype(jnp.float32) * weight).astype(jnp.bfloat16)
    split_gram(held_refs, scaled_ref, other_ref, 1)


def split_gram_kernel(back, scaled_ref, *refs):
    *held_refs, mine_ref = refs
    held_refs = [held_refs[i] for i in back]
    split_gram(held_refs, scaled_ref, mine_ref, 0)


def split_gram(held_refs, scaled_ref, out_ref, flip):
    index, column = lax.axis_index("tm"), lax.axis_index("col")
    place = lax.rem(lax.div(index, 2), 2)
    parity = jnp.bitwise_xor(lax.rem(index, 2), flip)
    all_refs, half_refs = held_refs[:2], held_refs[2:]
    groups, _, rows_out, length = half_refs[0].shape
    first = place * 2 * rows_out + parity * rows_out
    for block in range(2):
        total = None
        for unit in range(2):
            if block == 0:
                pieces = [
                    all_refs[unit][pl.ds(pl.multiple_of(g * 4 * rows_out + first, rows_out), rows_out), :]
                    for g in range(groups)
                ]
                rows = jnp.concatenate(pieces, axis=0)
            else:
                rows = half_refs[unit][:, parity].reshape(groups * rows_out, length)
            product = lax.dot_general(
                rows, scaled_ref[unit], (((1,), (1,)), ((), ())), preferred_element_type=jnp.float32
            )
            total = product if total is None else total + product
        at = jnp.bitwise_xor(column, block) * groups
        out_ref[pl.ds(at, groups)] = total.reshape(groups, rows_out, total.shape[1])


def early_kernel(every_ref, rows_ref, scaled_ref, other_ref, mine_ref):
    scaled_ref[...] = scaled_block(every_ref, rows_ref)
    for out_ref, flip in ((other_ref, 1), (mine_ref, 0)):
        out_ref[...] = product_of(whole_rows(every_ref, out_ref.shape[:2], flip), scaled_ref).reshape(out_ref.shape)


def late_kernel(
    beside_ref, both_ref, column_ref, rows_beside_ref, scaled_ref, early_ref, out_ref, scaled_beside_ref
):
    scaled_beside_ref[...] = scaled_block(beside_ref, rows_beside_ref)
    late_sums(1, beside_ref, both_ref, column_ref, scaled_ref, early_ref, scaled_beside_ref, out_ref)


def late_mine_kernel(*refs):
    late_sums(0, *refs)


def late_sums(flip, beside_ref, both_ref, column_ref, scaled_ref, early_ref, scaled_beside_ref, out_ref):
    groups, rows_out, width = early_ref.shape
    column = lax.axis_index("col")
    parity = jnp.bitwise_xor(lax.rem(lax.axis_index("tm"), 2), flip)
    same = product_of(whole_rows(beside_ref, (groups, rows_out), flip), scaled_beside_ref)
    out_ref[pl.ds(column * groups, groups)] = early_ref[...] + same.reshape(early_ref.shape)
    halves = [ref[:, parity].reshape(groups * rows_out, width) for ref in (column_ref, both_ref)]
    cross = product_of(halves[0], scaled_ref) + product_of(halves[1], scaled_beside_ref)
    out_ref[pl.ds((1 - column) * groups, groups)] = cross.reshape(early_ref.shape)


def scaled_block(block_ref, rows_ref):
    weight = jnp.concatenate([rows_ref[0:1], rows_ref[1:2]], axis=1)
    return (block_ref[...].astype(jnp.float32) * weight).astype(jnp.bfloat16)


def whole_rows(ref, shape, flip):
    groups, rows_out = shape
    index = lax.axis_index("tm")
    parity = jnp.bitwise_xor(lax.rem(index, 2), flip)
    first = (lax.rem(lax.div(index, 2), 2) * 2 + parity) * rows_out
    pieces = [
        ref[pl.ds(pl.multiple_of(g * 4 * rows_out + first, rows_out), rows_out), :] for g in range(groups)
    ]
    return jnp.concatenate(pieces, axis=0)


def product_of(rows, scaled_ref):
    return lax.dot_general(
        rows, scaled_ref[...], (((1,), (1,)), ((), ())), preferred_element_type=jnp.float32
    )


def scale_kernel(ids_ref, rows_ref, rows_beside_ref, *refs):
    *held_refs, other_ref, scaled_ref = refs
    columns = len(held_refs) // 2
    width, length = scaled_ref.shape[1:]
    column = lax.axis_index("col")
    for unit, ref in enumerate((rows_ref, rows_beside_ref)):
        weight = jnp.concatenate([ref[0:1], ref[1:2]], axis=1)
        for d in range(columns):

            @pl.when(ids_ref[lax.rem(column + d, columns)] == column)
            def _(d=d, unit=unit, weight=weight):
                values = held_refs[2 * d + unit][...].reshape(width, length).astype(jnp.float32)
                scaled_ref[unit] = (values * weight).astype(jnp.bfloat16)

    gram(ids_ref, held_refs, scaled_ref, other_ref, 1)


def gram_kernel(ids_ref, scaled_ref, *refs):
    *held_refs, mine_ref = refs
    gram(ids_ref, held_refs, scaled_ref, mine_ref, 0)


def gram(ids_ref, held_refs, scaled_ref, out_ref, flip):
    columns = len(held_refs) // 2
    index, column = lax.axis_index("tm"), lax.axis_index("col")
    beside = lax.rem(lax.div(index, 2), 2)
    parity = jnp.bitwise_xor(lax.rem(index, 2), flip)
    length = scaled_ref.shape[2]
    groups, _, _, rows_out, _ = held_refs[0].shape
    for d in range(columns):
        total = None
        for unit in range(2):
            rows = held_refs[2 * d + unit][:, beside, parity].reshape(groups * rows_out, length)
            product = lax.dot_general(
                rows, scaled_ref[unit], (((1,), (1,)), ((), ())), preferred_element_type=jnp.float32
            )
            total = product if total is None else total + product
        place = pl.ds(ids_ref[lax.rem(column + d, columns)] * groups, groups)
        out_ref[place] = total.reshape(groups, rows_out, total.shape[1])


def body(design, filter_taps, segment, valid_flags, weights, block_ids):
    row_count = design.shape[0]
    block_width = design.shape[2]
    tap_count = filter_taps.shape[2]
    seg_count = filter_taps.shape[0]
    devices = lax.axis_size("tm")
    columns = lax.axis_size("col")
    rows_out = columns * block_width // devices
    halo_depth = (tap_count - 2) // row_count + 1
    if halo_depth != 4 or devices % 4:
        raise ValueError("halo depth")
    index = lax.axis_index("tm")
    swap = [(i, i ^ 1) for i in range(devices)]
    beside_pairs = [(i, i ^ 2) for i in range(devices)]
    across_pairs = [(i, (i + (4 if i & 2 else -4)) % devices) for i in range(devices)]

    across = lax.ppermute(design, "tm", across_pairs)
    rows, ids = pl.pallas_call(
        rows_kernel,
        out_shape=[
            jax.ShapeDtypeStruct((8, row_count), jnp.float32),
            jax.ShapeDtypeStruct((1, columns), jnp.int32),
        ],
        in_specs=[VMEM] * 4,
        out_specs=[VMEM] * 2,
        compiler_params=LIMIT,
        name="rows",
    )(weights, valid_flags.reshape(1, row_count), segment.reshape(1, row_count), block_ids.reshape(1, columns))
    rows_pairs = [(i, i ^ 4 if i & 2 else (i - 4) % devices) for i in range(devices)]
    rows_across = lax.ppermute(rows, "tm", rows_pairs)
    beside = lax.ppermute(design, "tm", beside_pairs)
    spread, own = pl.pallas_call(
        prepare_kernel,
        out_shape=[
            jax.ShapeDtypeStruct((2 * seg_count, 2 * (halo_depth + 1) * row_count), jnp.bfloat16),
            jax.ShapeDtypeStruct(design.shape, design.dtype),
        ],
        in_specs=[VMEM] * 2,
        out_specs=[VMEM] * 2,
        compiler_params=LIMIT,
        name="prepare",
    )(filter_taps, design)
    toeplitz, rows_here = pl.pallas_call(
        toeplitz_kernel,
        out_shape=[
            jax.ShapeDtypeStruct((halo_depth + 1, 2 * row_count, 2 * row_count), jnp.bfloat16),
            jax.ShapeDtypeStruct(rows.shape, rows.dtype),
        ],
        in_specs=[VMEM] * 3,
        out_specs=[VMEM] * 2,
        compiler_params=LIMIT,
        cost_estimate=LONG,
        name="toeplitz",
    )(rows, rows_across, spread)
    chosen = pl.pallas_call(
        choose_kernel,
        out_shape=jax.ShapeDtypeStruct((2, *design.shape), design.dtype),
        in_specs=[VMEM] * 3,
        out_specs=VMEM,
        compiler_params=LIMIT,
        name="choose",
    )(across, own, beside)
    swapped = lax.ppermute(chosen, "tm", swap)
    partial = pl.pallas_call(
        partial_kernel,
        out_shape=jax.ShapeDtypeStruct((2 * row_count, block_width), jnp.float32),
        in_specs=[VMEM] * 4,
        out_specs=VMEM,
        compiler_params=LIMIT,
        name="partial",
    )(toeplitz, beside, own, across)
    split = columns == 2 and rows_out % 16 == 0 and block_width % (4 * rows_out) == 0
    finish = finish_two if split else finish_any
    total = finish(rows_here, (partial, toeplitz, swapped), ids.reshape(columns), rows_out, swap, beside_pairs)
    return total * (1.0 / (2.0 * row_count * devices))


def core_sum(mine, other, swap):
    return mine + lax.ppermute(other, "tm", swap)


def sum_over_groups(total, stride, turns=(3, 1, 2)):
    devices = lax.axis_size("tm")
    index = lax.axis_index("tm")
    left = total.shape[0]
    while left > 1:
        group = 4 if left % 4 == 0 else 2
        shares = total.reshape(left // group, group, *total.shape[1:])
        place = index // stride % group

        def share(j):
            return lax.dynamic_index_in_dim(shares, j, 1, keepdims=False)

        total = share(place)
        for d in turns if group == 4 else (1,):
            total = total + lax.ppermute(share(place ^ d), "tm", [(i, i ^ (d * stride)) for i in range(devices)])
        stride, left = stride * group, left // group
    return total[0]


def finish_two(rows_here, blocks, block_ids, rows_out, swap, beside_pairs):
    devices = lax.axis_size("tm")
    length, width = blocks[0].shape
    groups = width // rows_out // 4
    half = jax.ShapeDtypeStruct((groups, 2, rows_out, length), jnp.bfloat16)
    every, here, there = pl.pallas_call(
        filter_split_kernel,
        out_shape=[jax.ShapeDtypeStruct((width, length), jnp.bfloat16), half, half],
        in_specs=[VMEM] * 3,
        out_specs=[VMEM] * 3,
        compiler_params=LIMIT,
        name="filter",
    )(*blocks)

    def sums(own_block):
        def run(every, here, there, rows_here):
            across_column = [(0, 1), (1, 0)]
            both = [(i * 2 + c, (i ^ 2) * 2 + 1 - c) for i in range(devices) for c in range(2)]
            if own_block:
                held = (
                    every,
                    lax.ppermute(every, "tm", beside_pairs),
                    lax.ppermute(here, "col", across_column),
                    lax.ppermute(there, ("tm", "col"), both),
                )
            else:
                held = (
                    lax.ppermute(every, "col", across_column),
                    lax.ppermute(every, ("tm", "col"), both),
                    here,
                    lax.ppermute(there, "tm", beside_pairs),
                )
            order = (1, 3, 2, 0) if own_block else (3, 0, 1, 2)
            back = tuple(order.index(i) for i in range(4))
            share = jax.ShapeDtypeStruct((2 * groups, rows_out, width), jnp.float32)
            other, scaled = pl.pallas_call(
                functools.partial(split_scale_kernel, back),
                out_shape=[share, jax.ShapeDtypeStruct((2, width, length), jnp.bfloat16)],
                in_specs=[VMEM] * 6,
                out_specs=[VMEM] * 2,
                compiler_params=LIMIT,
                name="scale",
            )(*(held[i] for i in order), rows_here, lax.ppermute(rows_here, "tm", beside_pairs))
            mine = pl.pallas_call(
                functools.partial(split_gram_kernel, back),
                out_shape=share,
                in_specs=[VMEM] * 5,
                out_specs=VMEM,
                compiler_params=LIMIT,
                name="gram",
            )(scaled, *(held[i] for i in order))
            return sum_over_groups(core_sum(mine, other, swap), 4, (2, 1, 3) if own_block else (3, 1, 2))

        return run

    def sums_own(every, here, there, rows_here):
        beside_every = lax.ppermute(every, "tm", beside_pairs)
        column_half = lax.ppermute(here, "col", [(0, 1), (1, 0)])
        both = [(i * 2 + c, (i ^ 2) * 2 + 1 - c) for i in range(devices) for c in range(2)]
        both_half = lax.ppermute(there, ("tm", "col"), both)
        rows_beside = lax.ppermute(rows_here, "tm", beside_pairs)
        share = jax.ShapeDtypeStruct((groups, rows_out, width), jnp.float32)
        shares = jax.ShapeDtypeStruct((2 * groups, rows_out, width), jnp.float32)
        block = jax.ShapeDtypeStruct((width, length), jnp.bfloat16)
        scaled, other_early, mine_early = pl.pallas_call(
            early_kernel,
            out_shape=[block, share, share],
            in_specs=[VMEM] * 2,
            out_specs=[VMEM] * 3,
            compiler_params=LIMIT,
            name="early",
        )(every, rows_here)
        other, scaled_beside = pl.pallas_call(
            late_kernel,
            out_shape=[shares, block],
            in_specs=[VMEM] * 6,
            out_specs=[VMEM] * 2,
            compiler_params=LIMIT,
            name="late",
        )(beside_every, both_half, column_half, rows_beside, scaled, other_early)
        mine = pl.pallas_call(
            late_mine_kernel,
            out_shape=shares,
            in_specs=[VMEM] * 6,
            out_specs=VMEM,
            compiler_params=LIMIT,
            name="late_mine",
        )(beside_every, both_half, column_half, scaled, mine_early, scaled_beside)
        return sum_over_groups(core_sum(mine, other, swap), 4, (2, 1, 3))

    return lax.cond(block_ids[0] == 0, sums_own, sums(False), every, here, there, rows_here)


def finish_any(rows_here, blocks, block_ids, rows_out, swap, beside_pairs):
    devices, columns = lax.axis_size("tm"), lax.axis_size("col")
    length, width = blocks[0].shape
    filtered = pl.pallas_call(
        filter_kernel,
        out_shape=jax.ShapeDtypeStruct((width // rows_out // 4, 2, 2, rows_out, length), jnp.bfloat16),
        in_specs=[VMEM] * 3,
        out_specs=VMEM,
        compiler_params=LIMIT,
        name="filter",
    )(*blocks)
    held = []
    for d in range(columns):
        for e in range(2):
            pairs = [
                (i * columns + (c + d) % columns, (i ^ 2 * e) * columns + c)
                for i in range(devices)
                for c in range(columns)
            ]
            held.append(lax.ppermute(filtered, ("tm", "col"), pairs) if d or e else filtered)
    rows_beside = lax.ppermute(rows_here, "tm", beside_pairs)
    share = jax.ShapeDtypeStruct((devices // 4, rows_out, width), jnp.float32)
    other, scaled = pl.pallas_call(
        scale_kernel,
        out_shape=[share, jax.ShapeDtypeStruct((2, width, length), jnp.bfloat16)],
        in_specs=[SMEM] + [VMEM] * (2 + 2 * columns),
        out_specs=[VMEM] * 2,
        compiler_params=LIMIT,
        name="scale",
    )(block_ids, rows_here, rows_beside, *held)
    mine = pl.pallas_call(
        gram_kernel,
        out_shape=share,
        in_specs=[SMEM] + [VMEM] * (1 + 2 * columns),
        out_specs=VMEM,
        compiler_params=LIMIT,
        name="gram",
    )(block_ids, scaled, *held)
    return sum_over_groups(core_sum(mine, other, swap), 4)


def solution(mesh):
    return jax.shard_map(
        body,
        mesh=mesh,
        in_specs=(P("tm", None, "col"), P(), P("tm"), P("tm"), P(None, "tm"), P()),
        out_specs=P("tm", "col"),
        check_vma=False,
    )
```

```python
import functools

import jax
import jax.numpy as jnp
from jax import lax
from jax.experimental import pallas as pl
from jax.experimental.pallas import tpu as pltpu
from jax.sharding import PartitionSpec as P

VMEM = pl.BlockSpec(memory_space=pltpu.VMEM)
SMEM = pl.BlockSpec(memory_space=pltpu.SMEM)
FIRST = (((0,), (0,)), ((), ()))
LIMIT = pltpu.CompilerParams(vmem_limit_bytes=24 * 2**20)
LONG = pl.CostEstimate(flops=2 * 10**10, bytes_accessed=2**20, transcendentals=0)


def rows_kernel(weights_ref, flags_ref, segment_ref, ids_ref, rows_ref, ids_out_ref):
    ids_out_ref[...] = ids_ref[...]
    rows_ref[0:2, :] = weights_ref[...] * flags_ref[...].astype(jnp.float32)
    rows_ref[2:3, :] = segment_ref[...].astype(jnp.float32)
    rows_ref[3:, :] = jnp.zeros_like(rows_ref[3:, :])


def prepare_kernel(taps_ref, design_ref, spread_ref, own_ref):
    own_ref[...] = design_ref[...]
    seg_count, _, tap_count = taps_ref.shape
    width = spread_ref.shape[1]
    row_count = design_ref.shape[0]
    tile = 128
    lane = lax.broadcasted_iota(jnp.int32, (tile, 2 * tile), 1)
    row = lax.broadcasted_iota(jnp.int32, (tile, 2 * tile), 0)
    taps = taps_ref[...].reshape(2 * seg_count, tap_count)
    component = lax.rem(lax.broadcasted_iota(jnp.int32, (2 * seg_count, 2 * tile), 0), 2)
    flips = [(lane == 2 * (tile - 1 - row) + k).astype(jnp.float32).astype(jnp.bfloat16) for k in range(2)]
    pieces = []
    for place in range(tap_count - tile, -1, -tile):
        part = taps[:, place : place + tile]
        first, second = (jnp.dot(part, flip, preferred_element_type=jnp.float32) for flip in flips)
        pieces.append(jnp.where(component == 0, first, second))
    pieces.append(jnp.zeros((2 * seg_count, width - 2 * tap_count), jnp.float32))
    spread = pltpu.roll(jnp.concatenate(pieces, axis=1), width - 2 * row_count - 2 * (tap_count - 1), 1)
    spread_ref[...] = spread.astype(jnp.bfloat16)


def choose_kernel(across_ref, own_ref, beside_ref, out_ref):
    out_ref[1] = beside_ref[...]
    index = lax.axis_index("tm")
    both = jnp.bitwise_and(jnp.bitwise_xor(index, lax.div(index, 2)), 1)

    @pl.when(both == 0)
    def _():
        out_ref[0] = across_ref[...]

    @pl.when(both == 1)
    def _():
        out_ref[0] = own_ref[...]


def toeplitz_kernel(rows_ref, rows_across_ref, spread_ref, out_ref, rows_here_ref):
    sources, width = spread_ref.shape
    depth, _, step = out_ref.shape
    row_count = step // 2
    later, epoch_block = epoch_block_here()
    rows = jnp.where(later, rows_across_ref[...], rows_ref[...])
    rows_here_ref[...] = rows
    segment = 2 * rows[2:3, :].astype(jnp.int32)
    source = lax.broadcasted_iota(jnp.int32, (sources, row_count), 0)
    column = lax.broadcasted_iota(jnp.int32, (row_count, width), 1)
    first_column = 2 * ((depth - 1) - epoch_block) * row_count
    for k in range(2):
        selector = (source == segment + k).astype(jnp.float32).astype(jnp.bfloat16)
        shifted = lax.dot_general(selector, spread_ref[...], FIRST, preferred_element_type=jnp.float32)
        shifted = pltpu.roll(shifted, 0, 1, stride=2, stride_axis=0)
        shifted = jnp.where(column >= first_column, shifted, 0.0).astype(jnp.bfloat16)
        for d in range(depth):
            place = (depth - 1 - d) * step
            out_ref[d, k * row_count : (k + 1) * row_count, :] = shifted[:, place : place + step]


def epoch_block_here():
    index, devices = lax.axis_index("tm"), lax.axis_size("tm")
    later = lax.rem(lax.div(index, 2), 2) == 0
    return later, jnp.where(later, lax.rem(index + 4, devices), index)


def sum_products(toeplitz_ref, pairs, total=None):
    for d, block_ref in pairs:
        row_count, _, width = block_ref.shape
        block = block_ref[...].reshape(2 * row_count, width)
        product = jnp.dot(toeplitz_ref[d], block, preferred_element_type=jnp.float32)
        total = product if total is None else total + product
    return total


def partial_kernel(toeplitz_ref, beside_ref, own_ref, across_ref, out_ref):
    later, _ = epoch_block_here()
    back = jnp.where(later, 4, 0)
    out_ref[...] = sum_products(toeplitz_ref, ((2, beside_ref), (back, own_ref), (4 - back, across_ref)))


def filtered_block(partial_ref, toeplitz_ref, swapped_ref):
    odd = lax.rem(lax.axis_index("tm"), 2)
    pairs = ((1 + 2 * odd, swapped_ref.at[1]), (3 - 2 * odd, swapped_ref.at[0]))
    return sum_products(toeplitz_ref, pairs, partial_ref[...]).astype(jnp.bfloat16).T


def filter_kernel(partial_ref, toeplitz_ref, swapped_ref, out_ref):
    block = filtered_block(partial_ref, toeplitz_ref, swapped_ref)
    out_ref[...] = block.reshape(out_ref.shape)


def filter_split_kernel(partial_ref, toeplitz_ref, swapped_ref, all_ref, here_ref, there_ref):
    block = filtered_block(partial_ref, toeplitz_ref, swapped_ref)
    width, length = block.shape
    all_ref[...] = block
    groups, _, rows_out, _ = here_ref.shape
    block = block.reshape(groups, 2, 2, rows_out, length)
    place = lax.rem(lax.div(lax.axis_index("tm"), 2), 2)
    for side in range(2):

        @pl.when(place == side)
        def _(side=side):
            here_ref[...] = block[:, side]
            there_ref[...] = block[:, 1 - side]


def split_scale_kernel(back, *refs):
    *held_refs, rows_ref, rows_beside_ref, other_ref, scaled_ref = refs
    held_refs = [held_refs[i] for i in back]
    for unit, (ref, lines_ref) in enumerate(zip(held_refs[:2], (rows_ref, rows_beside_ref))):
        weight = jnp.concatenate([lines_ref[0:1], lines_ref[1:2]], axis=1)
        scaled_ref[unit] = (ref[...].astype(jnp.float32) * weight).astype(jnp.bfloat16)
    split_gram(held_refs, scaled_ref, other_ref, 1)


def split_gram_kernel(back, scaled_ref, *refs):
    *held_refs, mine_ref = refs
    held_refs = [held_refs[i] for i in back]
    split_gram(held_refs, scaled_ref, mine_ref, 0)


def split_gram(held_refs, scaled_ref, out_ref, flip):
    index, column = lax.axis_index("tm"), lax.axis_index("col")
    place = lax.rem(lax.div(index, 2), 2)
    parity = jnp.bitwise_xor(lax.rem(index, 2), flip)
    all_refs, half_refs = held_refs[:2], held_refs[2:]
    groups, _, rows_out, length = half_refs[0].shape
    first = place * 2 * rows_out + parity * rows_out
    for block in range(2):
        total = None
        for unit in range(2):
            if block == 0:
                pieces = [
                    all_refs[unit][pl.ds(pl.multiple_of(g * 4 * rows_out + first, rows_out), rows_out), :]
                    for g in range(groups)
                ]
                rows = jnp.concatenate(pieces, axis=0)
            else:
                rows = half_refs[unit][:, parity].reshape(groups * rows_out, length)
            product = lax.dot_general(
                rows, scaled_ref[unit], (((1,), (1,)), ((), ())), preferred_element_type=jnp.float32
            )
            total = product if total is None else total + product
        at = jnp.bitwise_xor(column, block) * groups
        out_ref[pl.ds(at, groups)] = total.reshape(groups, rows_out, total.shape[1])


def early_kernel(every_ref, rows_ref, scaled_ref, other_ref, mine_ref):
    scaled_ref[...] = scaled_block(every_ref, rows_ref)
    for out_ref, flip in ((other_ref, 1), (mine_ref, 0)):
        out_ref[...] = product_of(whole_rows(every_ref, out_ref.shape[:2], flip), scaled_ref).reshape(out_ref.shape)


def late_kernel(
    beside_ref, both_ref, column_ref, rows_beside_ref, scaled_ref, early_ref, out_ref, scaled_beside_ref
):
    scaled_beside_ref[...] = scaled_block(beside_ref, rows_beside_ref)
    late_sums(1, beside_ref, both_ref, column_ref, scaled_ref, early_ref, scaled_beside_ref, out_ref)


def late_mine_kernel(*refs):
    late_sums(0, *refs)


def late_sums(flip, beside_ref, both_ref, column_ref, scaled_ref, early_ref, scaled_beside_ref, out_ref):
    groups, rows_out, width = early_ref.shape
    column = lax.axis_index("col")
    parity = jnp.bitwise_xor(lax.rem(lax.axis_index("tm"), 2), flip)
    same = product_of(whole_rows(beside_ref, (groups, rows_out), flip), scaled_beside_ref)
    out_ref[pl.ds(column * groups, groups)] = early_ref[...] + same.reshape(early_ref.shape)
    halves = [ref[:, parity].reshape(groups * rows_out, width) for ref in (column_ref, both_ref)]
    cross = product_of(halves[0], scaled_ref) + product_of(halves[1], scaled_beside_ref)
    out_ref[pl.ds((1 - column) * groups, groups)] = cross.reshape(early_ref.shape)


def scaled_block(block_ref, rows_ref):
    weight = jnp.concatenate([rows_ref[0:1], rows_ref[1:2]], axis=1)
    return (block_ref[...].astype(jnp.float32) * weight).astype(jnp.bfloat16)


def whole_rows(ref, shape, flip):
    groups, rows_out = shape
    index = lax.axis_index("tm")
    parity = jnp.bitwise_xor(lax.rem(index, 2), flip)
    first = (lax.rem(lax.div(index, 2), 2) * 2 + parity) * rows_out
    pieces = [
        ref[pl.ds(pl.multiple_of(g * 4 * rows_out + first, rows_out), rows_out), :] for g in range(groups)
    ]
    return jnp.concatenate(pieces, axis=0)


def product_of(rows, scaled_ref):
    return lax.dot_general(
        rows, scaled_ref[...], (((1,), (1,)), ((), ())), preferred_element_type=jnp.float32
    )


def scale_kernel(ids_ref, rows_ref, rows_beside_ref, *refs):
    *held_refs, other_ref, scaled_ref = refs
    columns = len(held_refs) // 2
    width, length = scaled_ref.shape[1:]
    column = lax.axis_index("col")
    for unit, ref in enumerate((rows_ref, rows_beside_ref)):
        weight = jnp.concatenate([ref[0:1], ref[1:2]], axis=1)
        for d in range(columns):

            @pl.when(ids_ref[lax.rem(column + d, columns)] == column)
            def _(d=d, unit=unit, weight=weight):
                values = held_refs[2 * d + unit][...].reshape(width, length).astype(jnp.float32)
                scaled_ref[unit] = (values * weight).astype(jnp.bfloat16)

    gram(ids_ref, held_refs, scaled_ref, other_ref, 1)


def gram_kernel(ids_ref, scaled_ref, *refs):
    *held_refs, mine_ref = refs
    gram(ids_ref, held_refs, scaled_ref, mine_ref, 0)


def gram(ids_ref, held_refs, scaled_ref, out_ref, flip):
    columns = len(held_refs) // 2
    index, column = lax.axis_index("tm"), lax.axis_index("col")
    beside = lax.rem(lax.div(index, 2), 2)
    parity = jnp.bitwise_xor(lax.rem(index, 2), flip)
    length = scaled_ref.shape[2]
    groups, _, _, rows_out, _ = held_refs[0].shape
    for d in range(columns):
        total = None
        for unit in range(2):
            rows = held_refs[2 * d + unit][:, beside, parity].reshape(groups * rows_out, length)
            product = lax.dot_general(
                rows, scaled_ref[unit], (((1,), (1,)), ((), ())), preferred_element_type=jnp.float32
            )
            total = product if total is None else total + product
        place = pl.ds(ids_ref[lax.rem(column + d, columns)] * groups, groups)
        out_ref[place] = total.reshape(groups, rows_out, total.shape[1])


def body(design, filter_taps, segment, valid_flags, weights, block_ids):
    row_count = design.shape[0]
    block_width = design.shape[2]
    tap_count = filter_taps.shape[2]
    seg_count = filter_taps.shape[0]
    devices = lax.axis_size("tm")
    columns = lax.axis_size("col")
    rows_out = columns * block_width // devices
    halo_depth = (tap_count - 2) // row_count + 1
    if halo_depth != 4 or devices % 4:
        raise ValueError("halo depth")
    index = lax.axis_index("tm")
    swap = [(i, i ^ 1) for i in range(devices)]
    beside_pairs = [(i, i ^ 2) for i in range(devices)]
    across_pairs = [(i, (i + (4 if i & 2 else -4)) % devices) for i in range(devices)]

    across = lax.ppermute(design, "tm", across_pairs)
    rows, ids = pl.pallas_call(
        rows_kernel,
        out_shape=[
            jax.ShapeDtypeStruct((8, row_count), jnp.float32),
            jax.ShapeDtypeStruct((1, columns), jnp.int32),
        ],
        in_specs=[VMEM] * 4,
        out_specs=[VMEM] * 2,
        compiler_params=LIMIT,
        name="rows",
    )(weights, valid_flags.reshape(1, row_count), segment.reshape(1, row_count), block_ids.reshape(1, columns))
    rows_pairs = [(i, i ^ 4 if i & 2 else (i - 4) % devices) for i in range(devices)]
    rows_across = lax.ppermute(rows, "tm", rows_pairs)
    beside = lax.ppermute(design, "tm", beside_pairs)
    spread, own = pl.pallas_call(
        prepare_kernel,
        out_shape=[
            jax.ShapeDtypeStruct((2 * seg_count, 2 * (halo_depth + 1) * row_count), jnp.bfloat16),
            jax.ShapeDtypeStruct(design.shape, design.dtype),
        ],
        in_specs=[VMEM] * 2,
        out_specs=[VMEM] * 2,
        compiler_params=LIMIT,
        name="prepare",
    )(filter_taps, design)
    toeplitz, rows_here = pl.pallas_call(
        toeplitz_kernel,
        out_shape=[
            jax.ShapeDtypeStruct((halo_depth + 1, 2 * row_count, 2 * row_count), jnp.bfloat16),
            jax.ShapeDtypeStruct(rows.shape, rows.dtype),
        ],
        in_specs=[VMEM] * 3,
        out_specs=[VMEM] * 2,
        compiler_params=LIMIT,
        cost_estimate=LONG,
        name="toeplitz",
    )(rows, rows_across, spread)
    chosen = pl.pallas_call(
        choose_kernel,
        out_shape=jax.ShapeDtypeStruct((2, *design.shape), design.dtype),
        in_specs=[VMEM] * 3,
        out_specs=VMEM,
        compiler_params=LIMIT,
        name="choose",
    )(across, own, beside)
    swapped = lax.ppermute(chosen, "tm", swap)
    partial = pl.pallas_call(
        partial_kernel,
        out_shape=jax.ShapeDtypeStruct((2 * row_count, block_width), jnp.float32),
        in_specs=[VMEM] * 4,
        out_specs=VMEM,
        compiler_params=LIMIT,
        name="partial",
    )(toeplitz, beside, own, across)
    split = columns == 2 and rows_out % 16 == 0 and block_width % (4 * rows_out) == 0
    finish = finish_two if split else finish_any
    total = finish(rows_here, (partial, toeplitz, swapped), ids.reshape(columns), rows_out, swap, beside_pairs)
    return total


def core_sum(mine, other, swap):
    return mine + lax.ppermute(other, "tm", swap)


def sum_over_groups(total, stride, count, turns=(3, 1, 2)):
    devices = lax.axis_size("tm")
    index = lax.axis_index("tm")
    left = total.shape[0]
    while left > 1:
        group = 4 if left % 4 == 0 else 2
        shares = total.reshape(left // group, group, *total.shape[1:])
        place = index // stride % group

        def share(j):
            return lax.dynamic_index_in_dim(shares, j, 1, keepdims=False)

        total = share(place)
        for d in turns if group == 4 else (1,):
            total = total + lax.ppermute(share(place ^ d), "tm", [(i, i ^ (d * stride)) for i in range(devices)])
        stride, left = stride * group, left // group
    return total[0] * (1.0 / count)


def finish_two(rows_here, blocks, block_ids, rows_out, swap, beside_pairs):
    devices = lax.axis_size("tm")
    length, width = blocks[0].shape
    count = float(length * devices)
    groups = width // rows_out // 4
    half = jax.ShapeDtypeStruct((groups, 2, rows_out, length), jnp.bfloat16)
    every, here, there = pl.pallas_call(
        filter_split_kernel,
        out_shape=[jax.ShapeDtypeStruct((width, length), jnp.bfloat16), half, half],
        in_specs=[VMEM] * 3,
        out_specs=[VMEM] * 3,
        compiler_params=LIMIT,
        name="filter",
    )(*blocks)

    def sums(own_block):
        def run(every, here, there, rows_here):
            across_column = [(0, 1), (1, 0)]
            both = [(i * 2 + c, (i ^ 2) * 2 + 1 - c) for i in range(devices) for c in range(2)]
            if own_block:
                held = (
                    every,
                    lax.ppermute(every, "tm", beside_pairs),
                    lax.ppermute(here, "col", across_column),
                    lax.ppermute(there, ("tm", "col"), both),
                )
            else:
                held = (
                    lax.ppermute(every, "col", across_column),
                    lax.ppermute(every, ("tm", "col"), both),
                    here,
                    lax.ppermute(there, "tm", beside_pairs),
                )
            order = (1, 3, 2, 0) if own_block else (3, 0, 1, 2)
            back = tuple(order.index(i) for i in range(4))
            share = jax.ShapeDtypeStruct((2 * groups, rows_out, width), jnp.float32)
            other, scaled = pl.pallas_call(
                functools.partial(split_scale_kernel, back),
                out_shape=[share, jax.ShapeDtypeStruct((2, width, length), jnp.bfloat16)],
                in_specs=[VMEM] * 6,
                out_specs=[VMEM] * 2,
                compiler_params=LIMIT,
                name="scale",
            )(*(held[i] for i in order), rows_here, lax.ppermute(rows_here, "tm", beside_pairs))
            mine = pl.pallas_call(
                functools.partial(split_gram_kernel, back),
                out_shape=share,
                in_specs=[VMEM] * 5,
                out_specs=VMEM,
                compiler_params=LIMIT,
                name="gram",
            )(scaled, *(held[i] for i in order))
            return sum_over_groups(core_sum(mine, other, swap), 4, count, (2, 1, 3) if own_block else (3, 1, 2))

        return run

    def sums_own(every, here, there, rows_here):
        beside_every = lax.ppermute(every, "tm", beside_pairs)
        column_half = lax.ppermute(here, "col", [(0, 1), (1, 0)])
        both = [(i * 2 + c, (i ^ 2) * 2 + 1 - c) for i in range(devices) for c in range(2)]
        both_half = lax.ppermute(there, ("tm", "col"), both)
        rows_beside = lax.ppermute(rows_here, "tm", beside_pairs)
        share = jax.ShapeDtypeStruct((groups, rows_out, width), jnp.float32)
        shares = jax.ShapeDtypeStruct((2 * groups, rows_out, width), jnp.float32)
        block = jax.ShapeDtypeStruct((width, length), jnp.bfloat16)
        scaled, other_early, mine_early = pl.pallas_call(
            early_kernel,
            out_shape=[block, share, share],
            in_specs=[VMEM] * 2,
            out_specs=[VMEM] * 3,
            compiler_params=LIMIT,
            name="early",
        )(every, rows_here)
        other, scaled_beside = pl.pallas_call(
            late_kernel,
            out_shape=[shares, block],
            in_specs=[VMEM] * 6,
            out_specs=[VMEM] * 2,
            compiler_params=LIMIT,
            name="late",
        )(beside_every, both_half, column_half, rows_beside, scaled, other_early)
        mine = pl.pallas_call(
            late_mine_kernel,
            out_shape=shares,
            in_specs=[VMEM] * 6,
            out_specs=VMEM,
            compiler_params=LIMIT,
            name="late_mine",
        )(beside_every, both_half, column_half, scaled, mine_early, scaled_beside)
        return sum_over_groups(core_sum(mine, other, swap), 4, count, (2, 1, 3))

    return lax.cond(block_ids[0] == 0, sums_own, sums(False), every, here, there, rows_here)


def finish_any(rows_here, blocks, block_ids, rows_out, swap, beside_pairs):
    devices, columns = lax.axis_size("tm"), lax.axis_size("col")
    length, width = blocks[0].shape
    count = float(length * devices)
    filtered = pl.pallas_call(
        filter_kernel,
        out_shape=jax.ShapeDtypeStruct((width // rows_out // 4, 2, 2, rows_out, length), jnp.bfloat16),
        in_specs=[VMEM] * 3,
        out_specs=VMEM,
        compiler_params=LIMIT,
        name="filter",
    )(*blocks)
    held = []
    for d in range(columns):
        for e in range(2):
            pairs = [
                (i * columns + (c + d) % columns, (i ^ 2 * e) * columns + c)
                for i in range(devices)
                for c in range(columns)
            ]
            held.append(lax.ppermute(filtered, ("tm", "col"), pairs) if d or e else filtered)
    rows_beside = lax.ppermute(rows_here, "tm", beside_pairs)
    share = jax.ShapeDtypeStruct((devices // 4, rows_out, width), jnp.float32)
    other, scaled = pl.pallas_call(
        scale_kernel,
        out_shape=[share, jax.ShapeDtypeStruct((2, width, length), jnp.bfloat16)],
        in_specs=[SMEM] + [VMEM] * (2 + 2 * columns),
        out_specs=[VMEM] * 2,
        compiler_params=LIMIT,
        name="scale",
    )(block_ids, rows_here, rows_beside, *held)
    mine = pl.pallas_call(
        gram_kernel,
        out_shape=share,
        in_specs=[SMEM] + [VMEM] * (1 + 2 * columns),
        out_specs=VMEM,
        compiler_params=LIMIT,
        name="gram",
    )(block_ids, scaled, *held)
    return sum_over_groups(core_sum(mine, other, swap), 4, count)


def solution(mesh):
    return jax.shard_map(
        body,
        mesh=mesh,
        in_specs=(P("tm", None, "col"), P(), P("tm"), P("tm"), P(None, "tm"), P()),
        out_specs=P("tm", "col"),
        check_vma=False,
    )
```
